32 devices in a mesh: parts: 2 (over x), row: 2 (over core), col: 8 (over z, y).
Axes of the slice: x: 2, y: 2, z: 4, core: 2. Of those that a mesh axis runs over, the one named last changes fastest.
Arguments:
- hidden: bfloat16 [2048, 29568], P('parts', 'col'), parts along dimension 0, may hold values from -6 to 6
- cotangent: bfloat16 [2048, 8192], P(('parts', 'col'), 'row'), parts along dimension 0, may hold values from -6 to 6
- down_weight: bfloat16 [29568, 8192], P('col', 'row'), may hold values from -0.03125 to 0.03125
- adapter_a: bfloat16 [8, 16, 29568], P('parts', None, 'col'), parts along dimension 0, may hold values from -0.03125 to 0.03125
- adapter_b: bfloat16 [8, 16, 8192], P('parts', None, 'row'), parts along dimension 0, may hold values from -0.0625 to 0.0625
- seg_start: int32 [8], P('parts'), parts along dimension 0, may hold values from 0 to 896, as said below
- seg_len: int32 [8], P('parts'), parts along dimension 0, may hold values from 1 to 384, as said below
- tenant_slot: int32 [8], P('parts'), parts along dimension 0, may hold values from 0 to 3, each once
Outputs:
- hidden_gradient: bfloat16 [2048, 29568], P(('parts', 'row'), 'col'), parts along dimension 0
- grad_a: float32 [8, 16, 29568], P('parts', None, 'col'), parts along dimension 0
- grad_b: float32 [8, 16, 8192], P('parts', None, ('row', 'col')), parts along dimension 0
The draws below stay inside these ranges and needn't reach their ends.
There are 2 independent parts, one for each index of `parts`. The reference program is written for one: setup_inputs(seed, part) draws one part's arguments, and reference() takes and returns one part's arrays. A program takes and returns all parts, laid end to end along the dimension named above; an argument that names none is the same for every part. Nothing has to cross between parts.
Inputs may be any that keep to these rules, and one draw needn't show every extreme that they name: Starts are multiples of 128 and increase with the tenant; the first is 0, and tenant i's tiles are rows seg_start[i] up to the next tenant's start (the last tenant's up to 1024), so that every tenant holds one tile or more and the tiles cover all rows. The live rows of tenant i are the first seg_len[i] rows of its tiles; the rest of its last tile is padding. `tenant_slot`: each slot belongs to exactly one tenant.
All inputs are finite; a program needn't handle non-finite values.
Results may differ from the reference program's by a relative error of at most 0.012.
Values may be sent and summed in bfloat16 or wider, within the bound.
No kernel may reach another device: no remote copies, remote signals or barrier semaphores. Data moves between devices by JAX's collectives and lax.ppermute only.
A program may use at most 192 MiB of HBM per device.

```python
import jax
import jax.numpy as jnp

D = 8192
FF = 29568
R = 16
TILE = 128
TOKENS = 1024
TENANTS = 4


def tile_plan(key):
    biggest = max(2, TENANTS // 4)
    spread = TENANTS - biggest
    order = jax.random.permutation(jax.random.fold_in(key, 101), TENANTS).astype(jnp.int32)
    place = jnp.argsort(order).astype(jnp.int32)
    extra_tiles = jnp.where(place == 0, biggest, jnp.where(place <= spread, 1, 0)).astype(jnp.int32)
    tile_counts = 1 + extra_tiles
    padding = jax.random.randint(jax.random.fold_in(key, 102), (TENANTS,), 0, TILE)
    padding = jnp.where(place == 0, 0, padding).astype(jnp.int32)
    return (tile_counts, padding)


def draw_seg_start(key, part):
    tile_counts, padding = tile_plan(key)
    return ((jnp.cumsum(tile_counts) - tile_counts) * TILE).astype(jnp.int32)


def draw_seg_len(key, part):
    tile_counts, padding = tile_plan(key)
    return (tile_counts * TILE - padding).astype(jnp.int32)


def levels(own_key, extent, shards, least, top_value):
    factor_of = 1.0
    for position, blocks in shards:
        heights = jax.random.uniform(jax.random.fold_in(jax.random.fold_in(own_key, 6), position), (blocks,), jnp.float32, least / len(shards), top_value / len(shards))
        factor_of = factor_of * jnp.repeat(jnp.exp(heights), extent[position] // blocks).reshape((-1,) + (1,) * (len(extent) - 1 - position))
    return factor_of


def gaussian(key, dims, width, bound, cuts=(), held_as=jnp.bfloat16):
    loudness = levels(key, dims, cuts, -0.22, 0.18) if cuts else 1.0
    entries = jax.random.normal(key, dims, jnp.float32) * width * loudness
    return jnp.minimum(jnp.maximum(entries, -bound), bound).astype(held_as)


def setup_inputs(seed: int = 0, part: int = 0) -> dict:
    splits = jax.random.split(jax.random.key(seed), 9)
    part_keys = jax.random.split(jax.random.fold_in(splits[8], part), 9)
    hidden = gaussian(part_keys[0], (TOKENS, FF), 1.0, 6.0, ((1, 8),))
    cotangent = gaussian(part_keys[1], (TOKENS, D), 1.0, 6.0, ((0, 8), (1, 2)))
    down_weight = gaussian(splits[2], (FF, D), FF ** -0.5, 0.03125, ((0, 8), (1, 2)))
    adapter_a = gaussian(part_keys[3], (TENANTS, R, FF), FF ** -0.5, 0.03125, ((2, 8),))
    adapter_b = gaussian(part_keys[4], (TENANTS, R, D), D ** -0.5, 0.0625, ((2, 2),))
    seg_start = draw_seg_start(jax.random.fold_in(jax.random.fold_in(splits[8], part), 71), part)
    seg_len = draw_seg_len(jax.random.fold_in(jax.random.fold_in(splits[8], part), 71), part)
    tenant_slot = jax.random.permutation(part_keys[7], TENANTS).astype(jnp.int32)
    return dict(hidden=hidden, cotangent=cotangent, down_weight=down_weight, adapter_a=adapter_a, adapter_b=adapter_b, seg_start=seg_start, seg_len=seg_len, tenant_slot=tenant_slot)


adapter_scale_value = 4.0


def reference(hidden, cotangent, down_weight, adapter_a, adapter_b, seg_start, seg_len, tenant_slot):
    tokens_all = hidden.shape[0]
    tenants = seg_start.shape[0]
    rank_width = adapter_a.shape[1]
    rows_index = jnp.arange(tokens_all, dtype=jnp.int32)
    row_tenant = jnp.sum((rows_index[:, None] >= seg_start[None, :]).astype(jnp.int32), axis=1) - 1
    seg_end = seg_start + seg_len
    live_rows = rows_index < seg_end[row_tenant]
    row_slot = tenant_slot[row_tenant]
    masked = jnp.where(live_rows[:, None], cotangent, jnp.zeros_like(cotangent))
    slot_hot = (row_slot[:, None] == jnp.arange(tenants, dtype=jnp.int32)[None, :]).astype(jnp.float32)
    projection_flattened = adapter_a.reshape(tenants * rank_width, FF)
    back_flat = adapter_b.reshape(tenants * rank_width, D)
    low_all = jnp.dot(hidden, projection_flattened.T, preferred_element_type=jnp.float32).reshape(tokens_all, tenants, rank_width)
    low_rows = jnp.sum(low_all * slot_hot[:, :, None], axis=1).astype(jnp.bfloat16)
    back_all = jnp.dot(masked, back_flat.T, preferred_element_type=jnp.float32).reshape(tokens_all, tenants, rank_width)
    back_rows = jnp.sum(back_all * slot_hot[:, :, None], axis=1).astype(jnp.bfloat16)
    spread_gradient_back = (back_rows.astype(jnp.float32)[:, None, :] * slot_hot[:, :, None]).reshape(tokens_all, tenants * rank_width).astype(jnp.bfloat16)
    spread_low = (low_rows.astype(jnp.float32)[:, None, :] * slot_hot[:, :, None]).reshape(tokens_all, tenants * rank_width).astype(jnp.bfloat16)
    frozen_path = jnp.dot(masked, down_weight.T, preferred_element_type=jnp.float32)
    adapter_contribution = jnp.dot(spread_gradient_back, projection_flattened, preferred_element_type=jnp.float32)
    hidden_gradient = (frozen_path + adapter_scale_value * adapter_contribution).astype(jnp.bfloat16)
    slot_table = (tenant_slot[:, None] == jnp.arange(tenants, dtype=jnp.int32)[None, :]).astype(jnp.float32)
    tenant_slot_rows = jnp.sum(slot_table * seg_len.astype(jnp.float32)[:, None], axis=0)
    tenant_slot_factor = adapter_scale_value / tenant_slot_rows
    grad_a = jnp.dot(spread_gradient_back.T, hidden, preferred_element_type=jnp.float32).reshape(tenants, rank_width, FF)
    grad_a = grad_a * tenant_slot_factor[:, None, None]
    grad_b = jnp.dot(spread_low.T, masked, preferred_element_type=jnp.float32).reshape(tenants, rank_width, D)
    grad_b = grad_b * tenant_slot_factor[:, None, None]
    return hidden_gradient, grad_a, grad_b
```

```python
import functools

import jax
import jax.numpy as jnp
from jax import lax
from jax.experimental import pallas as pl
from jax.experimental.pallas import tpu as pltpu
from jax.sharding import PartitionSpec as P

TILE = 128


adapter_scale_value = 4.0

NT = (((1,), (1,)), ((), ()))
MIB = 1 << 20


def ring_order(n):
    return [2 * i for i in range(n // 2)] + [2 * i + 1 for i in reversed(range(n // 2))]


def col_at(n, k):
    col = lax.axis_index("col")
    line, side = col // 2, col % 2
    pos = jnp.where(side == 0, line, n - 1 - line)
    pos = lax.rem(pos + k + n, n)
    return jnp.where(pos < n // 2, 2 * pos, 2 * (n - 1 - pos) + 1)


def tile_facts(row0, start, length, slot):
    tenants = start.shape[0]
    found_slot, end = slot[0], start[0] + length[0]
    for i in range(1, tenants):
        here = start[i] <= row0
        found_slot = jnp.where(here, slot[i], found_slot)
        end = jnp.where(here, start[i] + length[i], end)
    return found_slot, end - row0


def put_tile(x_ext, at, data, row0, b_flat, scalars, width, back_out=None):
    rows = data.shape[0]
    tile0 = row0 // TILE * TILE
    slot, live = tile_facts(tile0, *scalars)
    keep = lax.broadcasted_iota(jnp.int32, (rows, 1), 0) < live - (row0 - tile0)
    x_ext[at : at + rows, :width] = jnp.where(keep, data, jnp.zeros_like(data))
    back = lax.dot_general(
        x_ext[at : at + rows, :width], b_flat, NT, preferred_element_type=jnp.float32
    )
    rank = b_flat.shape[0] // scalars[0].shape[0]
    lane = lax.broadcasted_iota(jnp.int32, back.shape, 1)
    mine = (lane >= slot * rank) & (lane < slot * rank + rank)
    spread = jnp.where(mine, back * adapter_scale_value, 0.0).astype(jnp.bfloat16)
    x_ext[at : at + rows, width : width + b_flat.shape[0]] = spread
    pad = x_ext.shape[1] - width - b_flat.shape[0]
    if pad:
        x_ext[at : at + rows, width + b_flat.shape[0] :] = jnp.zeros((rows, pad), jnp.bfloat16)


def first_kernel(
    n, start, length, slot, w_hbm, h_hbm, x_ref, a_ref, b_ref, w_ext, p_ref, z_ref, h_ref, x_ext, low_all, back_all, w_sem, h_sem
):
    ff, width = w_hbm.shape
    tenants, rank = a_ref.shape[0], a_ref.shape[1]
    flat = tenants * rank
    pieces = w_sem.shape[0]
    block = ff // pieces
    h_copy = pltpu.make_async_copy(h_hbm, h_ref, h_sem)
    h_copy.start()
    w_copies = [
        pltpu.make_async_copy(
            w_hbm.at[pl.ds(i * block, block)],
            w_ext.at[pl.ds(i * block, block), pl.ds(0, width)],
            w_sem.at[i],
        )
        for i in range(pieces)
    ]
    for c in w_copies:
        c.start()
    scalars = (start, length, slot)
    col = lax.axis_index("col")
    a_flat = a_ref[...].reshape(flat, ff)
    b_flat = b_ref[...].reshape(flat, width)
    w_ext[:, width : width + flat] = a_flat.T
    pad = w_ext.shape[1] - width - flat
    if pad:
        w_ext[:, width + flat :] = jnp.zeros((ff, pad), jnp.bfloat16)
    rows = x_ref.shape[0]
    put_tile(x_ext, 0, x_ref[...], col * rows, b_flat, scalars, width)
    back_all[...] = lax.dot_general(
        b_flat, x_ext[:, :width], NT, preferred_element_type=jnp.float32
    )
    own_slot, _ = tile_facts(col * rows, *scalars)
    z_ref[...] = jnp.zeros_like(z_ref)
    z_ref[rank:, pl.ds(pl.multiple_of(col * rows, TILE), rows)] = back_all[
        pl.ds(pl.multiple_of(own_slot * rank, rank), rank), :
    ]
    h_copy.wait()
    low_all[...] = jnp.dot(a_flat, h_ref[...], preferred_element_type=jnp.float32)
    for j in range(low_all.shape[1] // TILE):
        s, _ = tile_facts(j * TILE, *scalars)
        cols = slice(j * TILE, (j + 1) * TILE)
        z_ref[:rank, cols] = low_all[pl.ds(pl.multiple_of(s * rank, rank), rank), cols] * 0.5
    for i, c in enumerate(w_copies):
        c.wait()
        part = slice(i * block, (i + 1) * block)
        p_ref[part] = lax.dot_general(
            w_ext[part], x_ext[...], NT, preferred_element_type=jnp.float32
        ).astype(jnp.bfloat16)


def first(n, scalars, down_weight, hidden_t, cotangent, adapter_a, adapter_b):
    ff, width = down_weight.shape
    rows = cotangent.shape[0]
    tokens = hidden_t.shape[1]
    rank = adapter_a.shape[1]
    flat = adapter_a.shape[0] * rank
    wide = width + -(-flat // 128) * 128
    pieces = 7 if ff % (7 * 16) == 0 else 1
    smem = pl.BlockSpec(memory_space=pltpu.SMEM)
    vmem = pl.BlockSpec(memory_space=pltpu.VMEM)
    hbm = pl.BlockSpec(memory_space=pltpu.HBM)
    return pl.pallas_call(
        functools.partial(first_kernel, n),
        in_specs=[smem, smem, smem, hbm, hbm, vmem, vmem, vmem],
        out_specs=[vmem, vmem, vmem, vmem],
        out_shape=[
            pltpu.VMEM((ff, wide), jnp.bfloat16),
            jax.ShapeDtypeStruct((ff, rows), jnp.bfloat16),
            jax.ShapeDtypeStruct((2 * rank, tokens), jnp.float32),
            pltpu.VMEM((ff, tokens), jnp.bfloat16),
        ],
        scratch_shapes=[
            pltpu.VMEM((rows, wide), jnp.bfloat16),
            pltpu.VMEM((flat, tokens), jnp.float32),
            pltpu.VMEM((flat, rows), jnp.float32),
            pltpu.SemaphoreType.DMA((pieces,)),
            pltpu.SemaphoreType.DMA,
        ],
        compiler_params=pltpu.CompilerParams(vmem_limit_bytes=10 * MIB),
        cost_estimate=pl.CostEstimate(
            flops=2 * ff * width * rows, bytes_accessed=2 * ff * (width + tokens), transcendentals=0
        ),
        name="first",
    )(*scalars, down_weight, hidden_t, cotangent, adapter_a, adapter_b)


def pass_kernel(n, steps, start, length, slot, w_ext, b_ref, xa_ref, xb_ref, p_ref, x_ext):
    width = b_ref.shape[2]
    flat = b_ref.shape[0] * b_ref.shape[1]
    b_flat = b_ref[...].reshape(flat, width)
    scalars = (start, length, slot)
    rows = xa_ref.shape[0]
    ka, kb, shift = steps
    per = TILE if shift == 0 else rows * 2
    put_tile(x_ext, 0, xa_ref[...], col_at(n, ka) * per, b_flat, scalars, width)
    put_tile(x_ext, rows, xb_ref[...], col_at(n, kb) * per + shift, b_flat, scalars, width)
    ff = p_ref.shape[0]
    block = ff // 3
    for i in range(3):
        part = slice(i * block, (i + 1) * block)
        p_ref[part] = lax.dot_general(
            w_ext[part], x_ext[...], NT, preferred_element_type=jnp.float32
        ).astype(jnp.bfloat16)


def one_pass(n, steps, scalars, w_ext, adapter_b, xa, xb):
    ff, wide = w_ext.shape
    rows = xa.shape[0] + xb.shape[0]
    smem = pl.BlockSpec(memory_space=pltpu.SMEM)
    vmem = pl.BlockSpec(memory_space=pltpu.VMEM)
    return pl.pallas_call(
        functools.partial(pass_kernel, n, steps),
        in_specs=[smem, smem, smem, vmem, vmem, vmem, vmem],
        out_specs=vmem,
        out_shape=jax.ShapeDtypeStruct((ff, rows), jnp.bfloat16),
        scratch_shapes=[pltpu.VMEM((rows, wide), jnp.bfloat16)],
        compiler_params=pltpu.CompilerParams(vmem_limit_bytes=12 * MIB),
        cost_estimate=pl.CostEstimate(
            flops=2 * ff * wide * 256, bytes_accessed=2 * ff * rows, transcendentals=0
        ),
        name="part_pass",
    )(*scalars, pltpu.with_memory_space_constraint(w_ext, pltpu.VMEM), adapter_b, xa, xb)


def join_kernel(n, plan, *refs):
    count = len(plan)
    pairs, out, total, sem = refs[: 2 * count], refs[-3], refs[-2], refs[-1]
    row = lax.axis_index("row")
    for phase in (0, 1):
        for i, (k, lane) in enumerate(plan):
            col = col_at(n, k)
            at = lax.rem(col, n // 2) * TILE

            @pl.when(col // (n // 2) == row)
            def _():
                copy = pltpu.make_async_copy(
                    total.at[i], out.at[:, pl.ds(pl.multiple_of(at, TILE), TILE)], sem.at[i]
                )
                if phase == 0:
                    lanes = slice(lane, lane + TILE)
                    total[i] = (
                        pairs[2 * i][:, lanes].astype(jnp.float32)
                        + pairs[2 * i + 1][:, lanes].astype(jnp.float32)
                    ).astype(jnp.bfloat16)
                    copy.start()
                else:
                    copy.wait()


def join(n, plan, pairs, out, half_rows):
    ff = pairs[0].shape[0]
    vmem = pl.BlockSpec(memory_space=pltpu.VMEM)
    hbm = pl.BlockSpec(memory_space=pltpu.HBM)
    args = list(pairs)
    given = {}
    if out is not None:
        args.append(out)
        given = {len(args) - 1: 0}

    def body(*refs):
        used = refs[: len(pairs)] + refs[len(args) :]
        join_kernel(n, plan, *used)

    return pl.pallas_call(
        body,
        in_specs=[vmem] * len(pairs) + [hbm] * (out is not None),
        out_specs=hbm,
        out_shape=jax.ShapeDtypeStruct((ff, half_rows), jnp.bfloat16),
        scratch_shapes=[
            pltpu.VMEM((len(plan), ff, TILE), jnp.bfloat16),
            pltpu.SemaphoreType.DMA((len(plan),)),
        ],
        input_output_aliases=given,
        compiler_params=pltpu.CompilerParams(vmem_limit_bytes=18 * MIB),
        cost_estimate=pl.CostEstimate(
            flops=0, bytes_accessed=6 * ff * TILE * len(plan), transcendentals=0
        ),
        name="join_halves",
    )(*args)


def spread_rows(scratch, values, start, length, slot):
    rank = values.shape[0]
    scratch[...] = jnp.zeros_like(scratch)
    for j in range(values.shape[1] // TILE):
        s, _ = tile_facts(j * TILE, start, length, slot)
        cols = slice(j * TILE, (j + 1) * TILE)
        scratch[pl.ds(pl.multiple_of(s * rank, rank), rank), cols] = values[:, cols]


def scale_rows(out_ref, value, start, length, slot):
    rank = value.shape[0] // start.shape[0]
    row_slot = lax.broadcasted_iota(jnp.int32, (value.shape[0], 1), 0) // rank
    factor = jnp.zeros((value.shape[0], 1), jnp.float32)
    for i in range(start.shape[0]):
        one = jnp.full((value.shape[0], 1), length[i], jnp.int32).astype(jnp.float32)
        factor = jnp.where(row_slot == slot[i], adapter_scale_value / one, factor)
    out_ref[...] = value * factor


def grad_a_kernel(start, length, slot, z_ref, h_ref, out_ref, spread):
    rank = z_ref.shape[0] // 2
    spread_rows(spread, z_ref[rank:], start, length, slot)
    value = lax.dot_general(
        spread[...].astype(jnp.bfloat16), h_ref[...], NT, preferred_element_type=jnp.float32
    )
    scale_rows(out_ref, value, start, length, slot)


def grad_a_of(scalars, z, hidden_t, tenants, rank):
    ff, tokens = hidden_t.shape
    smem = pl.BlockSpec(memory_space=pltpu.SMEM)
    vmem = pl.BlockSpec(memory_space=pltpu.VMEM)
    return pl.pallas_call(
        grad_a_kernel,
        in_specs=[smem, smem, smem, vmem, vmem],
        out_specs=vmem,
        out_shape=jax.ShapeDtypeStruct((tenants * rank, ff), jnp.float32),
        scratch_shapes=[pltpu.VMEM((tenants * rank, tokens), jnp.float32)],
        compiler_params=pltpu.CompilerParams(vmem_limit_bytes=8 * MIB),
        cost_estimate=pl.CostEstimate(
            flops=2 * ff * tokens * 256, bytes_accessed=4 * 64 * ff, transcendentals=0
        ),
        name="grad_a",
    )(*scalars, z, pltpu.with_memory_space_constraint(hidden_t, pltpu.VMEM))


def grad_b_kernel(n, plan, start, length, slot, z_ref, *refs):
    blocks, out_ref, spread, x_ref, sem = refs[: len(plan)], refs[-4], refs[-3], refs[-2], refs[-1]
    rank = z_ref.shape[0] // 2
    width = x_ref.shape[1]
    at = pl.multiple_of(lax.axis_index("col") * width, width)
    copies = []
    for i, (k, shift) in enumerate(plan):
        rows = blocks[i].shape[0]
        to = pl.multiple_of(col_at(n, k) * TILE + shift, rows)
        copies.append(
            pltpu.make_async_copy(
                blocks[i].at[:, pl.ds(at, width)], x_ref.at[pl.ds(to, rows)], sem.at[i]
            )
        )
    for c in copies:
        c.start()
    spread_rows(spread, z_ref[:rank].astype(jnp.bfloat16).astype(jnp.float32), start, length, slot)
    tokens = spread.shape[1]
    row = lax.broadcasted_iota(jnp.int32, (1, tokens), 1)
    live = row < 0
    for i in range(start.shape[0]):
        live = live | ((row >= start[i]) & (row < start[i] + length[i]))
    low = jnp.where(live, spread[...], 0.0).astype(jnp.bfloat16)
    for c in copies:
        c.wait()
    value = jnp.dot(low, x_ref[...], preferred_element_type=jnp.float32)
    scale_rows(out_ref, value, start, length, slot)


def grad_b_of(n, scalars, z, plan, blocks, col_width, tenants):
    rank, tokens = z.shape[0] // 2, z.shape[1]
    smem = pl.BlockSpec(memory_space=pltpu.SMEM)
    vmem = pl.BlockSpec(memory_space=pltpu.VMEM)
    hbm = pl.BlockSpec(memory_space=pl.ANY)
    return pl.pallas_call(
        functools.partial(grad_b_kernel, n, plan),
        in_specs=[smem, smem, smem, vmem] + [hbm] * len(blocks),
        out_specs=vmem,
        out_shape=jax.ShapeDtypeStruct((tenants * rank, col_width), jnp.float32),
        scratch_shapes=[
            pltpu.VMEM((tenants * rank, tokens), jnp.float32),
            pltpu.VMEM((tokens, col_width), jnp.bfloat16),
            pltpu.SemaphoreType.DMA((len(blocks),)),
        ],
        compiler_params=pltpu.CompilerParams(vmem_limit_bytes=6 * MIB),
        cost_estimate=pl.CostEstimate(
            flops=2 * tokens * col_width * 256, bytes_accessed=4 * tokens * col_width, transcendentals=0
        ),
        name="grad_b",
    )(*scalars, z, *blocks)


def ring_shards(hidden, cotangent, down_weight, adapter_a, adapter_b, seg_start, seg_len, tenant_slot):
    n = lax.axis_size("col")
    tenants, rank = adapter_a.shape[0], adapter_a.shape[1]
    tokens, ff = hidden.shape
    half = cotangent.shape[0] // 2
    scalars = (seg_start, seg_len, tenant_slot)
    order = ring_order(n)
    onward = [(order[i], order[(i + 1) % n]) for i in range(n)]
    back = [(d, s) for s, d in onward]
    swap = [(0, 1), (1, 0)]

    up, down = [cotangent], [cotangent]
    for k in range(1, n // 2):
        up.append(lax.ppermute(up[-1], "col", onward))
        down.append(lax.ppermute(down[-1], "col", back))
    up.append(lax.ppermute(up[-1][:half], "col", onward))
    down.append(lax.ppermute(down[-1][half:], "col", back))

    w_ext, part, z, hidden_t = first(
        n, scalars, down_weight, hidden.T, cotangent, adapter_a, adapter_b
    )
    z = z + lax.ppermute(z, "row", swap)
    bit = 1
    while bit < n:
        z = z + lax.ppermute(z, "col", [(i, i ^ bit) for i in range(n)])
        bit *= 2

    sums = [(part, lax.ppermute(part, "row", swap), [(0, 0)])]
    for k in range(1, n // 2 + 1):
        last = k == n // 2
        part = one_pass(
            n, (-k, k, half if last else 0), scalars, w_ext, adapter_b, up[k], down[k]
        )
        places = [(k, 0)] if last else [(-k, 0), (k, TILE)]
        sums.append((part, lax.ppermute(part, "row", swap), places))

    out = None
    for group in (sums[: n // 2 - 1], sums[n // 2 - 1 :]):
        plan, pairs = [], []
        for own, other, places in group:
            for place in places:
                plan.append(place)
                pairs += [own, other]
        out = join(n, plan, pairs, out, tokens // lax.axis_size("row"))
    grad_a = grad_a_of(scalars, z, hidden_t, tenants, rank)
    plan, blocks = [(0, 0)], [cotangent]
    for k in range(1, n // 2 + 1):
        last = k == n // 2
        plan += [(-k, 0), (k, half if last else 0)]
        blocks += [up[k], down[k]]
    grad_b = grad_b_of(n, scalars, z, plan, blocks, cotangent.shape[1] // n, tenants)
    return (
        out.T,
        grad_a.reshape(tenants, rank, ff),
        grad_b.reshape(tenants, rank, -1),
    )


def shards(hidden, cotangent, *rest):
    n, rows = lax.axis_size("col"), cotangent.shape[0]
    if rows == TILE and n % 2 == 0 and n & (n - 1) == 0 and lax.axis_size("row") == 2:
        return ring_shards(hidden, cotangent, *rest)
    return plain_shards(hidden, cotangent, *rest)


def plain_shards(hidden, cotangent, down_weight, adapter_a, adapter_b, seg_start, seg_len, tenant_slot):
    tokens_all = hidden.shape[0]
    local_rows = cotangent.shape[0]
    tile_total = tokens_all // TILE
    tenants = seg_start.shape[0]
    rank_width = adapter_a.shape[1]
    slot_table = (tenant_slot[:, None] == jnp.arange(tenants, dtype=jnp.int32)[None, :]).astype(
        jnp.float32
    )
    tile_first = jnp.arange(tile_total, dtype=jnp.int32) * TILE
    tile_tenant = jnp.sum((tile_first[:, None] >= seg_start[None, :]).astype(jnp.int32), axis=1) - 1
    tenant_hot = (tile_tenant[:, None] == jnp.arange(tenants, dtype=jnp.int32)[None, :]).astype(
        jnp.float32
    )
    tile_slot = jnp.dot(tenant_hot, slot_table, precision=lax.Precision.HIGHEST)
    tenant_slot_rows = jnp.sum(slot_table * seg_len.astype(jnp.float32)[:, None], axis=0)
    tenant_slot_factor = adapter_scale_value / tenant_slot_rows
    offset = lax.axis_index("col") * local_rows
    my_rows = offset + jnp.arange(local_rows, dtype=jnp.int32)
    seg_end = seg_start + seg_len
    live_rows = jnp.any(
        (my_rows[:, None] >= seg_start[None, :]) & (my_rows[:, None] < seg_end[None, :]), axis=1
    )
    masked = jnp.where(live_rows[:, None], cotangent, jnp.zeros_like(cotangent))
    slot_pick = tile_slot.astype(jnp.bfloat16)
    proj_tiles = jnp.einsum(
        "js,srf->jrf", slot_pick, adapter_a, preferred_element_type=jnp.float32
    ).astype(jnp.bfloat16)
    back_tiles = jnp.einsum(
        "js,srd->jrd", slot_pick, adapter_b, preferred_element_type=jnp.float32
    ).astype(jnp.bfloat16)
    hidden_tiles = hidden.reshape(tile_total, TILE, hidden.shape[1])
    low_part = jnp.einsum(
        "jtf,jrf->jtr", hidden_tiles, proj_tiles, preferred_element_type=jnp.float32
    ).reshape(tokens_all, rank_width)
    low_rows = lax.psum(low_part.astype(jnp.bfloat16), "col")
    gathered = lax.all_gather(masked, "col", axis=0, tiled=True)
    grad_part = jnp.einsum(
        "jtd,jrd->jtr",
        gathered.reshape(tile_total, TILE, gathered.shape[1]),
        back_tiles,
        preferred_element_type=jnp.float32,
    ).reshape(tokens_all, rank_width)
    grad_rows = lax.psum(grad_part.astype(jnp.bfloat16), "row")
    half_rows = tokens_all // lax.axis_size("row")
    my_start = lax.axis_index("row") * half_rows
    frozen_path_sum = lax.psum_scatter(
        lax.dot_general(
            gathered, down_weight, (((1,), (1,)), ((), ())), preferred_element_type=jnp.float32
        ).astype(jnp.bfloat16),
        "row",
        scatter_dimension=0,
        tiled=True,
    ).astype(jnp.float32)
    grad_mine = lax.dynamic_slice_in_dim(grad_rows, my_start, half_rows, 0).reshape(
        half_rows // TILE, TILE, rank_width
    )
    proj_mine = lax.dynamic_slice_in_dim(proj_tiles, my_start // TILE, half_rows // TILE, 0)
    adapter_contribution = jnp.einsum(
        "jtr,jrf->jtf", grad_mine, proj_mine, preferred_element_type=jnp.float32
    ).reshape(half_rows, hidden.shape[1])
    hidden_gradient = (frozen_path_sum + adapter_scale_value * adapter_contribution).astype(
        jnp.bfloat16
    )
    grad_tiles = grad_rows.reshape(tile_total, TILE, rank_width)
    first_grad_tiles = jnp.einsum(
        "jtr,jtf->jrf", grad_tiles, hidden_tiles, preferred_element_type=jnp.float32
    )
    grad_a = (
        jnp.einsum("js,jrf->srf", tile_slot, first_grad_tiles, precision=lax.Precision.HIGHEST)
        * tenant_slot_factor[:, None, None]
    )
    col_width = cotangent.shape[1] // lax.axis_size("col")
    col_start = lax.axis_index("col") * col_width
    col_block = lax.dynamic_slice_in_dim(gathered, col_start, col_width, 1).reshape(
        tile_total, TILE, col_width
    )
    second_grad_tiles = jnp.einsum(
        "jtr,jtd->jrd",
        low_rows.reshape(tile_total, TILE, rank_width),
        col_block,
        preferred_element_type=jnp.float32,
    )
    grad_b = (
        jnp.einsum("js,jrd->srd", tile_slot, second_grad_tiles, precision=lax.Precision.HIGHEST)
        * tenant_slot_factor[:, None, None]
    )
    return (hidden_gradient, grad_a, grad_b)


def solution(mesh):
    placed = (
        P("parts", "col"),
        P(("parts", "col"), "row"),
        P("col", "row"),
        P("parts", None, "col"),
        P("parts", None, "row"),
        P("parts"),
        P("parts"),
        P("parts"),
    )
    return jax.shard_map(
        shards,
        mesh=mesh,
        in_specs=placed,
        out_specs=(
            P(("parts", "row"), "col"),
            P("parts", None, "col"),
            P("parts", None, ("row", "col")),
        ),
        check_vma=False,
    )
```

```python
import functools

import jax
import jax.numpy as jnp
from jax import lax
from jax.experimental import pallas as pl
from jax.experimental.pallas import tpu as pltpu
from jax.sharding import PartitionSpec as P

TILE = 128


adapter_scale_value = 4.0

NT = (((1,), (1,)), ((), ()))
MIB = 1 << 20


def far(x):
    return pltpu.with_memory_space_constraint(x, pltpu.HBM)


def near(x):
    return pltpu.with_memory_space_constraint(x, pltpu.VMEM)

LIM = 15
SMALL = pl.CostEstimate(flops=1, bytes_accessed=1, transcendentals=0)


def ring_order(n):
    return [2 * i for i in range(n // 2)] + [2 * i + 1 for i in reversed(range(n // 2))]


def col_at(n, k):
    col = lax.axis_index("col")
    line, side = col // 2, col % 2
    pos = jnp.where(side == 0, line, n - 1 - line)
    pos = lax.rem(pos + k + n, n)
    return jnp.where(pos < n // 2, 2 * pos, 2 * (n - 1 - pos) + 1)


def tile_facts(row0, start, length, slot):
    tenants = start.shape[0]
    found_slot, end = slot[0], start[0] + length[0]
    for i in range(1, tenants):
        here = start[i] <= row0
        found_slot = jnp.where(here, slot[i], found_slot)
        end = jnp.where(here, start[i] + length[i], end)
    return found_slot, end - row0


def put_tile(x_ext, at, data, row0, b_flat, scalars, width, back_out=None):
    rows = data.shape[0]
    tile0 = row0 // TILE * TILE
    slot, live = tile_facts(tile0, *scalars)
    keep = lax.broadcasted_iota(jnp.int32, (rows, 1), 0) < live - (row0 - tile0)
    x_ext[at : at + rows, :width] = jnp.where(keep, data, jnp.zeros_like(data))
    back = lax.dot_general(
        x_ext[at : at + rows, :width], b_flat, NT, preferred_element_type=jnp.float32
    )
    rank = b_flat.shape[0] // scalars[0].shape[0]
    lane = lax.broadcasted_iota(jnp.int32, back.shape, 1)
    mine = (lane >= slot * rank) & (lane < slot * rank + rank)
    spread = jnp.where(mine, back * adapter_scale_value, 0.0).astype(jnp.bfloat16)
    x_ext[at : at + rows, width : width + b_flat.shape[0]] = spread
    pad = x_ext.shape[1] - width - b_flat.shape[0]
    if pad:
        x_ext[at : at + rows, width + b_flat.shape[0] :] = jnp.zeros((rows, pad), jnp.bfloat16)


def low_kernel(start, length, slot, h_hbm, x_hbm, a_ref, b_ref, z_ref, x_ext, low_all, back_all, h_ref, x_ref, sem):
    tenants, rank, ff = a_ref.shape
    flat, width = tenants * rank, b_ref.shape[2]
    x_copy = pltpu.make_async_copy(x_hbm, x_ref, sem.at[0])
    h_copy = pltpu.make_async_copy(h_hbm, h_ref, sem.at[1])
    x_copy.start()
    h_copy.start()
    scalars = (start, length, slot)
    rows = x_ref.shape[0]
    row0 = lax.axis_index("col") * rows
    a_flat = a_ref[...].reshape(flat, ff)
    b_flat = b_ref[...].reshape(flat, width)
    own_slot, live = tile_facts(row0, *scalars)
    keep = lax.broadcasted_iota(jnp.int32, (rows, 1), 0) < live
    x_copy.wait()
    x_ext[...] = jnp.where(keep, x_ref[...], jnp.zeros_like(x_ref))
    back_all[...] = lax.dot_general(b_flat, x_ext[...], NT, preferred_element_type=jnp.float32)
    z_ref[...] = jnp.zeros_like(z_ref)
    z_ref[rank:, pl.ds(pl.multiple_of(row0, TILE), rows)] = back_all[
        pl.ds(pl.multiple_of(own_slot * rank, rank), rank), :
    ]
    h_copy.wait()
    low_all[...] = jnp.dot(a_flat, h_ref[...], preferred_element_type=jnp.float32)
    for j in range(low_all.shape[1] // TILE):
        s, _ = tile_facts(j * TILE, *scalars)
        cols = slice(j * TILE, (j + 1) * TILE)
        z_ref[:rank, cols] = low_all[pl.ds(pl.multiple_of(s * rank, rank), rank), cols] * 0.5


def low_and_back(scalars, hidden_t, cotangent, adapter_a, adapter_b):
    ff, tokens = hidden_t.shape
    rows, width = cotangent.shape
    rank = adapter_a.shape[1]
    flat = adapter_a.shape[0] * rank
    smem = pl.BlockSpec(memory_space=pltpu.SMEM)
    vmem = pl.BlockSpec(memory_space=pltpu.VMEM)
    hbm = pl.BlockSpec(memory_space=pltpu.HBM)
    return pl.pallas_call(
        low_kernel,
        in_specs=[smem, smem, smem, hbm, hbm, vmem, vmem],
        out_specs=vmem,
        out_shape=jax.ShapeDtypeStruct((2 * rank, tokens), jnp.float32),
        scratch_shapes=[
            pltpu.VMEM((rows, width), jnp.bfloat16),
            pltpu.VMEM((flat, tokens), jnp.float32),
            pltpu.VMEM((flat, rows), jnp.float32),
            pltpu.VMEM((ff, tokens), jnp.bfloat16),
            pltpu.VMEM((rows, width), jnp.bfloat16),
            pltpu.SemaphoreType.DMA((2,)),
        ],
        compiler_params=pltpu.CompilerParams(vmem_limit_bytes=LIM * MIB),
        cost_estimate=SMALL,
        name="low_and_back",
    )(*[far(v) for v in scalars], far(hidden_t), far(cotangent), far(adapter_a), far(adapter_b))


def load_kernel(w_hbm, a_ref, w_ext, w_sem):
    ff, width = w_hbm.shape
    pieces = w_sem.shape[0]
    block = ff // pieces
    w_copies = [
        pltpu.make_async_copy(
            w_hbm.at[pl.ds(i * block, block)],
            w_ext.at[pl.ds(i * block, block), pl.ds(0, width)],
            w_sem.at[i],
        )
        for i in range(pieces)
    ]
    for c in w_copies:
        c.start()
    flat = a_ref.shape[0] * a_ref.shape[1]
    w_ext[:, width : width + flat] = a_ref[...].reshape(flat, ff).T
    pad = w_ext.shape[1] - width - flat
    if pad:
        w_ext[:, width + flat :] = jnp.zeros((ff, pad), jnp.bfloat16)
    for c in w_copies:
        c.wait()


def load(down_weight, adapter_a):
    ff, width = down_weight.shape
    flat = adapter_a.shape[0] * adapter_a.shape[1]
    wide = width + -(-flat // 128) * 128
    pieces = 7 if ff % (7 * 16) == 0 else 1
    return pl.pallas_call(
        load_kernel,
        in_specs=[
            pl.BlockSpec(memory_space=pltpu.HBM),
            pl.BlockSpec(memory_space=pltpu.VMEM),
        ],
        out_specs=pl.BlockSpec(memory_space=pltpu.VMEM),
        out_shape=pltpu.VMEM((ff, wide), jnp.bfloat16),
        scratch_shapes=[pltpu.SemaphoreType.DMA((pieces,))],
        compiler_params=pltpu.CompilerParams(vmem_limit_bytes=LIM * MIB),
        cost_estimate=SMALL,
        name="load_weight",
    )(down_weight, far(adapter_a))


def add_kernel(x_ref, y_ref, _, out_ref):
    out_ref[...] = x_ref[...] + y_ref[...]


def add_after(x, y, keep):
    vmem = pl.BlockSpec(memory_space=pltpu.VMEM)
    return pl.pallas_call(
        add_kernel,
        in_specs=[vmem, vmem, vmem],
        out_specs=vmem,
        out_shape=jax.ShapeDtypeStruct(x.shape, x.dtype),
        compiler_params=pltpu.CompilerParams(vmem_limit_bytes=LIM * MIB),
        cost_estimate=SMALL,
        name="add_after",
    )(x, y, near(keep))


def pass_kernel(n, steps, start, length, slot, w_ext, b_ref, *refs):
    xs, p_ref, x_ext = refs[: len(steps)], refs[-2], refs[-1]
    width = b_ref.shape[2]
    flat = b_ref.shape[0] * b_ref.shape[1]
    b_flat = b_ref[...].reshape(flat, width)
    at = 0
    for (k, shift), x_ref in zip(steps, xs):
        row0 = col_at(n, k) * TILE + shift
        put_tile(x_ext, at, x_ref[...], row0, b_flat, (start, length, slot), width)
        at += x_ref.shape[0]
    ff = p_ref.shape[0]
    block = ff // 3
    for i in range(3):
        part = slice(i * block, (i + 1) * block)
        p_ref[part] = lax.dot_general(
            w_ext[part], x_ext[...], NT, preferred_element_type=jnp.float32
        ).astype(jnp.bfloat16)


def one_pass(n, steps, scalars, w_ext, adapter_b, *xs):
    ff, wide = w_ext.shape
    rows = sum(x.shape[0] for x in xs)
    smem = pl.BlockSpec(memory_space=pltpu.SMEM)
    vmem = pl.BlockSpec(memory_space=pltpu.VMEM)
    return pl.pallas_call(
        functools.partial(pass_kernel, n, steps),
        in_specs=[smem, smem, smem] + [vmem] * (2 + len(xs)),
        out_specs=vmem,
        out_shape=jax.ShapeDtypeStruct((ff, rows), jnp.bfloat16),
        scratch_shapes=[pltpu.VMEM((rows, wide), jnp.bfloat16)],
        compiler_params=pltpu.CompilerParams(vmem_limit_bytes=LIM * MIB),
        cost_estimate=SMALL,
        name="part_pass",
    )(*scalars, near(w_ext), adapter_b, *xs)


def join_kernel(n, plan, in_vmem, *refs):
    out, parts, sem = refs[-3], refs[-2], refs[-1]
    row = lax.axis_index("row")

    def put_of(i, at):
        return pltpu.make_async_copy(parts.at[i, 0], out.at[:, pl.ds(at, TILE)], sem.at[i, 2])

    def fetch_of(i, own, other):
        return [
            pltpu.make_async_copy(src, parts.at[i, j], sem.at[i, j])
            for j, src in enumerate((own, other))
        ]

    def mine(body):
        for i, (pair, k, lane) in enumerate(plan):
            col = col_at(n, k)
            at = pl.multiple_of(lax.rem(col, n // 2) * TILE, TILE)
            lanes = pl.ds(lane, TILE)
            own, other = refs[2 * pair].at[:, lanes], refs[2 * pair + 1].at[:, lanes]
            pl.when(col // (n // 2) == row)(functools.partial(body, i, own, other, at))

    def begin(i, own, other, at):
        for c in fetch_of(i, own, other):
            c.start()

    def add(i, own, other, at):
        if in_vmem:
            a, b = own[...], other[...]
        else:
            for c in fetch_of(i, own, other):
                c.wait()
            a, b = parts[i, 0], parts[i, 1]
        parts[i, 0] = (a.astype(jnp.float32) + b.astype(jnp.float32)).astype(jnp.bfloat16)
        put_of(i, at).start()

    def end(i, own, other, at):
        put_of(i, at).wait()

    if not in_vmem:
        mine(begin)
    mine(add)
    mine(end)


def join(n, groups, out, half_rows, keep=None):
    ff = groups[0][0].shape[0]
    vmem = pl.BlockSpec(memory_space=pltpu.VMEM)
    hbm = pl.BlockSpec(memory_space=pltpu.HBM)
    in_vmem = keep is None
    args, plan, given = [], [], {}
    for pair, (own, other, places) in enumerate(groups):
        args += [own, other] if in_vmem else [far(own), far(other)]
        plan += [(pair, k, lane) for k, lane in places]
    count = len(args)
    specs = [vmem if in_vmem else hbm] * count
    if out is not None:
        given = {count: 0}
        args.append(out)
        specs.append(hbm)
    if keep is not None:
        args.append(near(keep))
        specs.append(vmem)

    def body(*refs):
        join_kernel(n, plan, in_vmem, *refs[:count], *refs[len(args) :])

    return pl.pallas_call(
        body,
        in_specs=specs,
        out_specs=hbm,
        out_shape=jax.ShapeDtypeStruct((ff, half_rows), jnp.bfloat16),
        scratch_shapes=[
            pltpu.VMEM((len(plan), 1 if in_vmem else 2, ff, TILE), jnp.bfloat16),
            pltpu.SemaphoreType.DMA((len(plan), 3)),
        ],
        input_output_aliases=given,
        compiler_params=pltpu.CompilerParams(vmem_limit_bytes=LIM * MIB),
        cost_estimate=SMALL,
        name="join_halves",
    )(*args)


def spread_rows(scratch, values, start, length, slot):
    rank = values.shape[0]
    scratch[...] = jnp.zeros_like(scratch)
    for j in range(values.shape[1] // TILE):
        s, _ = tile_facts(j * TILE, start, length, slot)
        cols = slice(j * TILE, (j + 1) * TILE)
        scratch[pl.ds(pl.multiple_of(s * rank, rank), rank), cols] = values[:, cols]


def scale_rows(out_ref, value, start, length, slot):
    rank = value.shape[0] // start.shape[0]
    row_slot = lax.broadcasted_iota(jnp.int32, (value.shape[0], 1), 0) // rank
    factor = jnp.zeros((value.shape[0], 1), jnp.float32)
    for i in range(start.shape[0]):
        one = jnp.full((value.shape[0], 1), length[i], jnp.int32).astype(jnp.float32)
        factor = jnp.where(row_slot == slot[i], adapter_scale_value / one, factor)
    out_ref[...] = value * factor


def grad_a_kernel(start, length, slot, z_ref, h_ref, out_ref, spread):
    rank = z_ref.shape[0] // 2
    spread_rows(spread, z_ref[rank:], start, length, slot)
    value = lax.dot_general(
        spread[...].astype(jnp.bfloat16), h_ref[...], NT, preferred_element_type=jnp.float32
    )
    scale_rows(out_ref, value, start, length, slot)


def grad_a_of(scalars, z, hidden_t, tenants, rank):
    ff, tokens = hidden_t.shape
    smem = pl.BlockSpec(memory_space=pltpu.SMEM)
    vmem = pl.BlockSpec(memory_space=pltpu.VMEM)
    return pl.pallas_call(
        grad_a_kernel,
        in_specs=[smem, smem, smem, vmem, vmem],
        out_specs=vmem,
        out_shape=jax.ShapeDtypeStruct((tenants * rank, ff), jnp.float32),
        scratch_shapes=[pltpu.VMEM((tenants * rank, tokens), jnp.float32)],
        compiler_params=pltpu.CompilerParams(vmem_limit_bytes=LIM * MIB),
        cost_estimate=SMALL,
        name="grad_a",
    )(*scalars, z, hidden_t)


def grad_b_kernel(n, plan, start, length, slot, z_ref, *refs):
    blocks, out_ref, spread, x_ref, sem = refs[: len(plan)], refs[-4], refs[-3], refs[-2], refs[-1]
    rank = z_ref.shape[0] // 2
    width = x_ref.shape[1]
    at = pl.multiple_of(lax.axis_index("col") * width, width)
    copies = []
    for i, (k, shift) in enumerate(plan):
        rows = blocks[i].shape[0]
        to = pl.multiple_of(col_at(n, k) * TILE + shift, rows)
        copies.append(
            pltpu.make_async_copy(
                blocks[i].at[:, pl.ds(at, width)], x_ref.at[pl.ds(to, rows)], sem.at[i]
            )
        )
    for c in copies:
        c.start()
    spread_rows(spread, z_ref[:rank].astype(jnp.bfloat16).astype(jnp.float32), start, length, slot)
    tokens = spread.shape[1]
    row = lax.broadcasted_iota(jnp.int32, (1, tokens), 1)
    live = row < 0
    for i in range(start.shape[0]):
        live = live | ((row >= start[i]) & (row < start[i] + length[i]))
    low = jnp.where(live, spread[...], 0.0).astype(jnp.bfloat16)
    for c in copies:
        c.wait()
    value = jnp.dot(low, x_ref[...], preferred_element_type=jnp.float32)
    scale_rows(out_ref, value, start, length, slot)


def grad_b_of(n, scalars, z, plan, blocks, col_width, tenants):
    rank, tokens = z.shape[0] // 2, z.shape[1]
    smem = pl.BlockSpec(memory_space=pltpu.SMEM)
    vmem = pl.BlockSpec(memory_space=pltpu.VMEM)
    hbm = pl.BlockSpec(memory_space=pl.ANY)
    return pl.pallas_call(
        functools.partial(grad_b_kernel, n, plan),
        in_specs=[smem, smem, smem, vmem] + [hbm] * len(blocks),
        out_specs=vmem,
        out_shape=jax.ShapeDtypeStruct((tenants * rank, col_width), jnp.float32),
        scratch_shapes=[
            pltpu.VMEM((tenants * rank, tokens), jnp.float32),
            pltpu.VMEM((tokens, col_width), jnp.bfloat16),
            pltpu.SemaphoreType.DMA((len(blocks),)),
        ],
        compiler_params=pltpu.CompilerParams(vmem_limit_bytes=LIM * MIB),
        cost_estimate=SMALL,
        name="grad_b",
    )(*scalars, z, *blocks)


def ring_shards(hidden, cotangent, down_weight, adapter_a, adapter_b, seg_start, seg_len, tenant_slot):
    n = lax.axis_size("col")
    tenants, rank = adapter_a.shape[0], adapter_a.shape[1]
    tokens, ff = hidden.shape
    half = cotangent.shape[0] // 2
    scalars = (seg_start, seg_len, tenant_slot)
    order = ring_order(n)
    onward = [(order[i], order[(i + 1) % n]) for i in range(n)]
    back = [(d, s) for s, d in onward]
    swap = [(0, 1), (1, 0)]

    def send(k):
        u, d = up[-1], down[-1]
        if k == n // 2:
            u, d = u[:half], d[half:]
        return lax.ppermute(u, "col", onward), lax.ppermute(d, "col", back)

    def hold(values):
        leaves, tree = jax.tree.flatten(values)
        at = [i for i, v in enumerate(leaves) if hasattr(v, "dtype")]
        held = lax.optimization_barrier([leaves[i] for i in at])
        for i, v in zip(at, held):
            leaves[i] = v
        return jax.tree.unflatten(tree, leaves)

    half_rows = tokens // lax.axis_size("row")
    hidden_t = hidden.T
    up, down = [cotangent], [cotangent]
    arrived = send(1)
    z = low_and_back(scalars, hidden_t, cotangent, adapter_a, adapter_b)
    moved = lax.ppermute(z, "row", swap)
    down_weight, z = hold((down_weight, z))
    w_ext = load(down_weight, adapter_a)
    z = add_after(z, moved, w_ext)
    def swap_z(z, bit):
        return lax.ppermute(z, "col", [(i, i ^ bit) for i in range(n)])

    moved, bit = swap_z(z, 1), 2
    arrived, z, moved = hold((arrived, z, moved))
    z = z + moved
    out, part, waiting = None, None, []
    for k in range(1, n // 2):
        up.append(arrived[0])
        down.append(arrived[1])
        arrived = send(k + 1)
        moved = None
        if 1 < k < n // 2 - 1 and bit < n // 2:
            moved, bit = swap_z(z, bit), bit * 2
        if part is not None:
            waiting.append((part, lax.ppermute(part, "row", swap), places))
        steps, blocks = [(-k, 0), (k, 0)], [up[k], down[k]]
        if k == 1:
            steps, blocks = [(0, 0)] + steps, [far(cotangent)] + blocks
        part = one_pass(n, steps, scalars, w_ext, adapter_b, *blocks)
        places = [(where, i * TILE) for i, (where, _) in enumerate(steps)]
        if k == 2:
            out = join(n, waiting, out, half_rows, w_ext)
            waiting = []
        arrived, part, z, moved, out, waiting = hold((arrived, part, z, moved, out, waiting))
        if moved is not None:
            z = z + moved
    up.append(arrived[0])
    down.append(arrived[1])
    while bit < n:
        z, bit = z + swap_z(z, bit), bit * 2
    waiting.append((part, lax.ppermute(part, "row", swap), places))
    part = one_pass(
        n, [(n // 2, 0), (n // 2, half)], scalars, w_ext, adapter_b, up[-1], down[-1]
    )
    part, z, waiting = hold((part, z, waiting))
    waiting.append((part, lax.ppermute(part, "row", swap), [(n // 2, 0)]))
    grad_a = grad_a_of(scalars, z, hidden_t, tenants, rank)
    plan, blocks = [(0, 0)], [cotangent]
    for k in range(1, n // 2 + 1):
        last = k == n // 2
        plan += [(-k, 0), (k, half if last else 0)]
        blocks += [up[k], down[k]]
    grad_b = grad_b_of(n, scalars, z, plan, blocks, cotangent.shape[1] // n, tenants)
    for group in (waiting[:-1], waiting[-1:]):
        out = join(n, group, out, half_rows)
    return (
        out.T,
        grad_a.reshape(tenants, rank, ff),
        grad_b.reshape(tenants, rank, -1),
    )


def shards(hidden, cotangent, *rest):
    n, rows = lax.axis_size("col"), cotangent.shape[0]
    if rows == TILE and n % 2 == 0 and n & (n - 1) == 0 and lax.axis_size("row") == 2:
        return ring_shards(hidden, cotangent, *rest)
    return plain_shards(hidden, cotangent, *rest)


def plain_shards(hidden, cotangent, down_weight, adapter_a, adapter_b, seg_start, seg_len, tenant_slot):
    tokens_all = hidden.shape[0]
    local_rows = cotangent.shape[0]
    tile_total = tokens_all // TILE
    tenants = seg_start.shape[0]
    rank_width = adapter_a.shape[1]
    slot_table = (tenant_slot[:, None] == jnp.arange(tenants, dtype=jnp.int32)[None, :]).astype(
        jnp.float32
    )
    tile_first = jnp.arange(tile_total, dtype=jnp.int32) * TILE
    tile_tenant = jnp.sum((tile_first[:, None] >= seg_start[None, :]).astype(jnp.int32), axis=1) - 1
    tenant_hot = (tile_tenant[:, None] == jnp.arange(tenants, dtype=jnp.int32)[None, :]).astype(
        jnp.float32
    )
    tile_slot = jnp.dot(tenant_hot, slot_table, precision=lax.Precision.HIGHEST)
    tenant_slot_rows = jnp.sum(slot_table * seg_len.astype(jnp.float32)[:, None], axis=0)
    tenant_slot_factor = adapter_scale_value / tenant_slot_rows
    offset = lax.axis_index("col") * local_rows
    my_rows = offset + jnp.arange(local_rows, dtype=jnp.int32)
    seg_end = seg_start + seg_len
    live_rows = jnp.any(
        (my_rows[:, None] >= seg_start[None, :]) & (my_rows[:, None] < seg_end[None, :]), axis=1
    )
    masked = jnp.where(live_rows[:, None], cotangent, jnp.zeros_like(cotangent))
    slot_pick = tile_slot.astype(jnp.bfloat16)
    proj_tiles = jnp.einsum(
        "js,srf->jrf", slot_pick, adapter_a, preferred_element_type=jnp.float32
    ).astype(jnp.bfloat16)
    back_tiles = jnp.einsum(
        "js,srd->jrd", slot_pick, adapter_b, preferred_element_type=jnp.float32
    ).astype(jnp.bfloat16)
    hidden_tiles = hidden.reshape(tile_total, TILE, hidden.shape[1])
    low_part = jnp.einsum(
        "jtf,jrf->jtr", hidden_tiles, proj_tiles, preferred_element_type=jnp.float32
    ).reshape(tokens_all, rank_width)
    low_rows = lax.psum(low_part.astype(jnp.bfloat16), "col")
    gathered = lax.all_gather(masked, "col", axis=0, tiled=True)
    grad_part = jnp.einsum(
        "jtd,jrd->jtr",
        gathered.reshape(tile_total, TILE, gathered.shape[1]),
        back_tiles,
        preferred_element_type=jnp.float32,
    ).reshape(tokens_all, rank_width)
    grad_rows = lax.psum(grad_part.astype(jnp.bfloat16), "row")
    half_rows = tokens_all // lax.axis_size("row")
    my_start = lax.axis_index("row") * half_rows
    frozen_path_sum = lax.psum_scatter(
        lax.dot_general(
            gathered, down_weight, (((1,), (1,)), ((), ())), preferred_element_type=jnp.float32
        ).astype(jnp.bfloat16),
        "row",
        scatter_dimension=0,
        tiled=True,
    ).astype(jnp.float32)
    grad_mine = lax.dynamic_slice_in_dim(grad_rows, my_start, half_rows, 0).reshape(
        half_rows // TILE, TILE, rank_width
    )
    proj_mine = lax.dynamic_slice_in_dim(proj_tiles, my_start // TILE, half_rows // TILE, 0)
    adapter_contribution = jnp.einsum(
        "jtr,jrf->jtf", grad_mine, proj_mine, preferred_element_type=jnp.float32
    ).reshape(half_rows, hidden.shape[1])
    hidden_gradient = (frozen_path_sum + adapter_scale_value * adapter_contribution).astype(
        jnp.bfloat16
    )
    grad_tiles = grad_rows.reshape(tile_total, TILE, rank_width)
    first_grad_tiles = jnp.einsum(
        "jtr,jtf->jrf", grad_tiles, hidden_tiles, preferred_element_type=jnp.float32
    )
    grad_a = (
        jnp.einsum("js,jrf->srf", tile_slot, first_grad_tiles, precision=lax.Precision.HIGHEST)
        * tenant_slot_factor[:, None, None]
    )
    col_width = cotangent.shape[1] // lax.axis_size("col")
    col_start = lax.axis_index("col") * col_width
    col_block = lax.dynamic_slice_in_dim(gathered, col_start, col_width, 1).reshape(
        tile_total, TILE, col_width
    )
    second_grad_tiles = jnp.einsum(
        "jtr,jtd->jrd",
        low_rows.reshape(tile_total, TILE, rank_width),
        col_block,
        preferred_element_type=jnp.float32,
    )
    grad_b = (
        jnp.einsum("js,jrd->srd", tile_slot, second_grad_tiles, precision=lax.Precision.HIGHEST)
        * tenant_slot_factor[:, None, None]
    )
    return (hidden_gradient, grad_a, grad_b)


def solution(mesh):
    placed = (
        P("parts", "col"),
        P(("parts", "col"), "row"),
        P("col", "row"),
        P("parts", None, "col"),
        P("parts", None, "row"),
        P("parts"),
        P("parts"),
        P("parts"),
    )
    return jax.shard_map(
        shards,
        mesh=mesh,
        in_specs=placed,
        out_specs=(
            P(("parts", "row"), "col"),
            P("parts", None, "col"),
            P("parts", None, ("row", "col")),
        ),
        check_vma=False,
    )
```

```python
import functools

import jax
import jax.numpy as jnp
from jax import lax
from jax.experimental import pallas as pl
from jax.experimental.pallas import tpu as pltpu
from jax.sharding import PartitionSpec as P

TILE = 128


adapter_scale_value = 4.0

NT = (((1,), (1,)), ((), ()))
MIB = 1 << 20


def far(x):
    return pltpu.with_memory_space_constraint(x, pltpu.HBM)


def near(x):
    return pltpu.with_memory_space_constraint(x, pltpu.VMEM)

LIM = 13
SMALL = pl.CostEstimate(flops=1, bytes_accessed=1, transcendentals=0)


def ring_order(n):
    return [2 * i for i in range(n // 2)] + [2 * i + 1 for i in reversed(range(n // 2))]


def col_at(n, k):
    col = lax.axis_index("col")
    line, side = col // 2, col % 2
    pos = jnp.where(side == 0, line, n - 1 - line)
    pos = lax.rem(pos + k + n, n)
    return jnp.where(pos < n // 2, 2 * pos, 2 * (n - 1 - pos) + 1)


def tile_facts(row0, start, length, slot):
    tenants = start.shape[0]
    found_slot, end = slot[0], start[0] + length[0]
    for i in range(1, tenants):
        here = start[i] <= row0
        found_slot = jnp.where(here, slot[i], found_slot)
        end = jnp.where(here, start[i] + length[i], end)
    return found_slot, end - row0


def put_tile(x_ext, at, data, row0, b_flat, scalars, width, back_out=None):
    rows = data.shape[0]
    tile0 = row0 // TILE * TILE
    slot, live = tile_facts(tile0, *scalars)
    keep = lax.broadcasted_iota(jnp.int32, (rows, 1), 0) < live - (row0 - tile0)
    x_ext[at : at + rows, :width] = jnp.where(keep, data, jnp.zeros_like(data))
    back = lax.dot_general(
        x_ext[at : at + rows, :width], b_flat, NT, preferred_element_type=jnp.float32
    )
    rank = b_flat.shape[0] // scalars[0].shape[0]
    lane = lax.broadcasted_iota(jnp.int32, back.shape, 1)
    mine = (lane >= slot * rank) & (lane < slot * rank + rank)
    spread = jnp.where(mine, back * adapter_scale_value, 0.0).astype(jnp.bfloat16)
    x_ext[at : at + rows, width : width + b_flat.shape[0]] = spread
    pad = x_ext.shape[1] - width - b_flat.shape[0]
    if pad:
        x_ext[at : at + rows, width + b_flat.shape[0] :] = jnp.zeros((rows, pad), jnp.bfloat16)


def low_kernel(start, length, slot, h_hbm, x_hbm, a_ref, b_ref, z_ref, x_ext, low_all, back_all, h_ref, x_ref, sem):
    tenants, rank, ff = a_ref.shape
    flat, width = tenants * rank, b_ref.shape[2]
    x_copy = pltpu.make_async_copy(x_hbm, x_ref, sem.at[0])
    h_copy = pltpu.make_async_copy(h_hbm, h_ref, sem.at[1])
    x_copy.start()
    h_copy.start()
    scalars = (start, length, slot)
    rows = x_ref.shape[0]
    row0 = lax.axis_index("col") * rows
    a_flat = a_ref[...].reshape(flat, ff)
    b_flat = b_ref[...].reshape(flat, width)
    own_slot, live = tile_facts(row0, *scalars)
    keep = lax.broadcasted_iota(jnp.int32, (rows, 1), 0) < live
    x_copy.wait()
    x_ext[...] = jnp.where(keep, x_ref[...], jnp.zeros_like(x_ref))
    back_all[...] = lax.dot_general(b_flat, x_ext[...], NT, preferred_element_type=jnp.float32)
    z_ref[...] = jnp.zeros_like(z_ref)
    z_ref[rank:, pl.ds(pl.multiple_of(row0, TILE), rows)] = back_all[
        pl.ds(pl.multiple_of(own_slot * rank, rank), rank), :
    ]
    h_copy.wait()
    low_all[...] = jnp.dot(a_flat, h_ref[...], preferred_element_type=jnp.float32)
    for j in range(low_all.shape[1] // TILE):
        s, _ = tile_facts(j * TILE, *scalars)
        cols = slice(j * TILE, (j + 1) * TILE)
        z_ref[:rank, cols] = low_all[pl.ds(pl.multiple_of(s * rank, rank), rank), cols] * 0.5


def low_and_back(scalars, hidden_t, cotangent, adapter_a, adapter_b):
    ff, tokens = hidden_t.shape
    rows, width = cotangent.shape
    rank = adapter_a.shape[1]
    flat = adapter_a.shape[0] * rank
    smem = pl.BlockSpec(memory_space=pltpu.SMEM)
    vmem = pl.BlockSpec(memory_space=pltpu.VMEM)
    hbm = pl.BlockSpec(memory_space=pltpu.HBM)
    return pl.pallas_call(
        low_kernel,
        in_specs=[smem, smem, smem, hbm, hbm, vmem, vmem],
        out_specs=vmem,
        out_shape=jax.ShapeDtypeStruct((2 * rank, tokens), jnp.float32),
        scratch_shapes=[
            pltpu.VMEM((rows, width), jnp.bfloat16),
            pltpu.VMEM((flat, tokens), jnp.float32),
            pltpu.VMEM((flat, rows), jnp.float32),
            pltpu.VMEM((ff, tokens), jnp.bfloat16),
            pltpu.VMEM((rows, width), jnp.bfloat16),
            pltpu.SemaphoreType.DMA((2,)),
        ],
        compiler_params=pltpu.CompilerParams(vmem_limit_bytes=LIM * MIB),
        cost_estimate=SMALL,
        name="low_and_back",
    )(*[far(v) for v in scalars], far(hidden_t), far(cotangent), far(adapter_a), far(adapter_b))


def load_kernel(w_hbm, a_ref, w_ext, w_sem):
    ff, width = w_hbm.shape
    pieces = w_sem.shape[0]
    block = ff // pieces
    w_copies = [
        pltpu.make_async_copy(
            w_hbm.at[pl.ds(i * block, block)],
            w_ext.at[pl.ds(i * block, block), pl.ds(0, width)],
            w_sem.at[i],
        )
        for i in range(pieces)
    ]
    for c in w_copies:
        c.start()
    flat = a_ref.shape[0] * a_ref.shape[1]
    w_ext[:, width : width + flat] = a_ref[...].reshape(flat, ff).T
    pad = w_ext.shape[1] - width - flat
    if pad:
        w_ext[:, width + flat :] = jnp.zeros((ff, pad), jnp.bfloat16)
    for c in w_copies:
        c.wait()


def load(down_weight, adapter_a):
    ff, width = down_weight.shape
    flat = adapter_a.shape[0] * adapter_a.shape[1]
    wide = width + -(-flat // 128) * 128
    pieces = 7 if ff % (7 * 16) == 0 else 1
    return pl.pallas_call(
        load_kernel,
        in_specs=[
            pl.BlockSpec(memory_space=pltpu.HBM),
            pl.BlockSpec(memory_space=pltpu.VMEM),
        ],
        out_specs=pl.BlockSpec(memory_space=pltpu.VMEM),
        out_shape=pltpu.VMEM((ff, wide), jnp.bfloat16),
        scratch_shapes=[pltpu.SemaphoreType.DMA((pieces,))],
        compiler_params=pltpu.CompilerParams(vmem_limit_bytes=LIM * MIB),
        cost_estimate=SMALL,
        name="load_weight",
    )(down_weight, far(adapter_a))


def add_kernel(x_ref, y_ref, _, out_ref):
    out_ref[...] = (x_ref[...] + y_ref[...]).astype(out_ref.dtype)


def add_after(x, y, keep):
    vmem = pl.BlockSpec(memory_space=pltpu.VMEM)
    return pl.pallas_call(
        add_kernel,
        in_specs=[vmem, vmem, vmem],
        out_specs=vmem,
        out_shape=jax.ShapeDtypeStruct(x.shape, jnp.bfloat16),
        compiler_params=pltpu.CompilerParams(vmem_limit_bytes=LIM * MIB),
        cost_estimate=SMALL,
        name="add_after",
    )(x, y, near(keep))


def pass_kernel(n, steps, start, length, slot, w_ext, b_ref, *refs):
    xs, p_ref, x_ext = refs[: len(steps)], refs[-2], refs[-1]
    width = b_ref.shape[2]
    flat = b_ref.shape[0] * b_ref.shape[1]
    b_flat = b_ref[...].reshape(flat, width)
    at = 0
    for (k, shift), x_ref in zip(steps, xs):
        row0 = col_at(n, k) * TILE + shift
        put_tile(x_ext, at, x_ref[...], row0, b_flat, (start, length, slot), width)
        at += x_ref.shape[0]
    ff = p_ref.shape[0]
    block = ff // 3
    for i in range(3):
        part = slice(i * block, (i + 1) * block)
        p_ref[part] = lax.dot_general(
            w_ext[part], x_ext[...], NT, preferred_element_type=jnp.float32
        ).astype(jnp.bfloat16)


def one_pass(n, steps, scalars, w_ext, adapter_b, *xs):
    ff, wide = w_ext.shape
    rows = sum(x.shape[0] for x in xs)
    smem = pl.BlockSpec(memory_space=pltpu.SMEM)
    vmem = pl.BlockSpec(memory_space=pltpu.VMEM)
    return pl.pallas_call(
        functools.partial(pass_kernel, n, steps),
        in_specs=[smem, smem, smem] + [vmem] * (2 + len(xs)),
        out_specs=vmem,
        out_shape=jax.ShapeDtypeStruct((ff, rows), jnp.bfloat16),
        scratch_shapes=[pltpu.VMEM((rows, wide), jnp.bfloat16)],
        compiler_params=pltpu.CompilerParams(vmem_limit_bytes=LIM * MIB),
        cost_estimate=SMALL,
        name="part_pass",
    )(*scalars, near(w_ext), adapter_b, *xs)


def join_kernel(n, plan, in_vmem, *refs):
    out, parts, sem = refs[-3], refs[-2], refs[-1]
    row = lax.axis_index("row")

    def put_of(i, at):
        return pltpu.make_async_copy(parts.at[i, 0], out.at[:, pl.ds(at, TILE)], sem.at[i, 2])

    def fetch_of(i, own, other):
        return [
            pltpu.make_async_copy(src, parts.at[i, j], sem.at[i, j])
            for j, src in enumerate((own, other))
        ]

    def mine(body):
        for i, (pair, k, lane) in enumerate(plan):
            col = col_at(n, k)
            at = pl.multiple_of(lax.rem(col, n // 2) * TILE, TILE)
            lanes = pl.ds(lane, TILE)
            own, other = refs[2 * pair].at[:, lanes], refs[2 * pair + 1].at[:, lanes]
            pl.when(col // (n // 2) == row)(functools.partial(body, i, own, other, at))

    def begin(i, own, other, at):
        for c in fetch_of(i, own, other):
            c.start()

    def add(i, own, other, at):
        if in_vmem:
            a, b = own[...], other[...]
        else:
            for c in fetch_of(i, own, other):
                c.wait()
            a, b = parts[i, 0], parts[i, 1]
        parts[i, 0] = (a.astype(jnp.float32) + b.astype(jnp.float32)).astype(jnp.bfloat16)
        put_of(i, at).start()

    def end(i, own, other, at):
        put_of(i, at).wait()

    if not in_vmem:
        mine(begin)
    mine(add)
    mine(end)


def join(n, groups, out, half_rows, keep=None, in_vmem=False):
    ff = groups[0][0].shape[0]
    vmem = pl.BlockSpec(memory_space=pltpu.VMEM)
    hbm = pl.BlockSpec(memory_space=pltpu.HBM)
    args, plan, given = [], [], {}
    for pair, (own, other, places) in enumerate(groups):
        args += [own, other]
        plan += [(pair, k, lane) for k, lane in places]
    count = len(args)
    specs = [vmem if in_vmem else pl.BlockSpec(memory_space=pl.ANY)] * count
    if out is not None:
        given = {count: 0}
        args.append(out)
        specs.append(hbm)
    if keep is not None:
        args.append(near(keep))
        specs.append(vmem)

    def body(*refs):
        join_kernel(n, plan, in_vmem, *refs[:count], *refs[len(args) :])

    return pl.pallas_call(
        body,
        in_specs=specs,
        out_specs=hbm,
        out_shape=jax.ShapeDtypeStruct((ff, half_rows), jnp.bfloat16),
        scratch_shapes=[
            pltpu.VMEM((len(plan), 1 if in_vmem else 2, ff, TILE), jnp.bfloat16),
            pltpu.SemaphoreType.DMA((len(plan), 3)),
        ],
        input_output_aliases=given,
        compiler_params=pltpu.CompilerParams(vmem_limit_bytes=LIM * MIB),
        cost_estimate=SMALL,
        name="join_halves",
    )(*args)


def spread_rows(scratch, values, start, length, slot):
    rank = values.shape[0]
    scratch[...] = jnp.zeros_like(scratch)
    for j in range(values.shape[1] // TILE):
        s, _ = tile_facts(j * TILE, start, length, slot)
        cols = slice(j * TILE, (j + 1) * TILE)
        scratch[pl.ds(pl.multiple_of(s * rank, rank), rank), cols] = values[:, cols]


def scale_rows(out_ref, value, start, length, slot):
    rank = value.shape[0] // start.shape[0]
    row_slot = lax.broadcasted_iota(jnp.int32, (value.shape[0], 1), 0) // rank
    factor = jnp.zeros((value.shape[0], 1), jnp.float32)
    for i in range(start.shape[0]):
        one = jnp.full((value.shape[0], 1), length[i], jnp.int32).astype(jnp.float32)
        factor = jnp.where(row_slot == slot[i], adapter_scale_value / one, factor)
    out_ref[...] = value * factor


def grad_a_kernel(start, length, slot, z_ref, h_ref, out_ref, spread):
    rank = z_ref.shape[0] // 2
    spread_rows(spread, z_ref[rank:].astype(jnp.float32), start, length, slot)
    value = lax.dot_general(
        spread[...].astype(jnp.bfloat16), h_ref[...], NT, preferred_element_type=jnp.float32
    )
    scale_rows(out_ref, value, start, length, slot)


def grad_a_of(scalars, z, hidden_t, tenants, rank):
    ff, tokens = hidden_t.shape
    smem = pl.BlockSpec(memory_space=pltpu.SMEM)
    vmem = pl.BlockSpec(memory_space=pltpu.VMEM)
    return pl.pallas_call(
        grad_a_kernel,
        in_specs=[smem, smem, smem, vmem, vmem],
        out_specs=vmem,
        out_shape=jax.ShapeDtypeStruct((tenants * rank, ff), jnp.float32),
        scratch_shapes=[pltpu.VMEM((tenants * rank, tokens), jnp.float32)],
        compiler_params=pltpu.CompilerParams(vmem_limit_bytes=LIM * MIB),
        cost_estimate=SMALL,
        name="grad_a",
    )(*scalars, z, hidden_t)


def grad_b_kernel(n, plan, start, length, slot, z_ref, *refs):
    blocks, out_ref, spread, x_ref, sem = refs[: len(plan)], refs[-4], refs[-3], refs[-2], refs[-1]
    rank = z_ref.shape[0] // 2
    width = x_ref.shape[1]
    at = pl.multiple_of(lax.axis_index("col") * width, width)
    copies = []
    for i, (k, shift) in enumerate(plan):
        rows = blocks[i].shape[0]
        to = pl.multiple_of(col_at(n, k) * TILE + shift, rows)
        copies.append(
            pltpu.make_async_copy(
                blocks[i].at[:, pl.ds(at, width)], x_ref.at[pl.ds(to, rows)], sem.at[i]
            )
        )
    for c in copies:
        c.start()
    spread_rows(spread, z_ref[:rank].astype(jnp.float32), start, length, slot)
    tokens = spread.shape[1]
    row = lax.broadcasted_iota(jnp.int32, (1, tokens), 1)
    live = row < 0
    for i in range(start.shape[0]):
        live = live | ((row >= start[i]) & (row < start[i] + length[i]))
    low = jnp.where(live, spread[...], 0.0).astype(jnp.bfloat16)
    for c in copies:
        c.wait()
    value = jnp.dot(low, x_ref[...], preferred_element_type=jnp.float32)
    scale_rows(out_ref, value, start, length, slot)


def grad_b_of(n, scalars, z, plan, blocks, col_width, tenants):
    rank, tokens = z.shape[0] // 2, z.shape[1]
    smem = pl.BlockSpec(memory_space=pltpu.SMEM)
    vmem = pl.BlockSpec(memory_space=pltpu.VMEM)
    hbm = pl.BlockSpec(memory_space=pl.ANY)
    return pl.pallas_call(
        functools.partial(grad_b_kernel, n, plan),
        in_specs=[smem, smem, smem, vmem] + [hbm] * len(blocks),
        out_specs=vmem,
        out_shape=jax.ShapeDtypeStruct((tenants * rank, col_width), jnp.float32),
        scratch_shapes=[
            pltpu.VMEM((tenants * rank, tokens), jnp.float32),
            pltpu.VMEM((tokens, col_width), jnp.bfloat16),
            pltpu.SemaphoreType.DMA((len(blocks),)),
        ],
        compiler_params=pltpu.CompilerParams(vmem_limit_bytes=LIM * MIB),
        cost_estimate=SMALL,
        name="grad_b",
    )(*scalars, z, *blocks)


def ring_shards(hidden, cotangent, down_weight, adapter_a, adapter_b, seg_start, seg_len, tenant_slot):
    n = lax.axis_size("col")
    tenants, rank = adapter_a.shape[0], adapter_a.shape[1]
    tokens, ff = hidden.shape
    half = cotangent.shape[0] // 2
    scalars = (seg_start, seg_len, tenant_slot)
    order = ring_order(n)
    onward = [(order[i], order[(i + 1) % n]) for i in range(n)]
    back = [(d, s) for s, d in onward]
    swap = [(0, 1), (1, 0)]

    def send(k):
        u, d = up[-1], down[-1]
        if k == n // 2:
            u, d = u[:half], d[half:]
        return lax.ppermute(u, "col", onward), lax.ppermute(d, "col", back)

    def hold(values):
        leaves, tree = jax.tree.flatten(values)
        at = [i for i, v in enumerate(leaves) if hasattr(v, "dtype")]
        held = lax.optimization_barrier([leaves[i] for i in at])
        for i, v in zip(at, held):
            leaves[i] = v
        return jax.tree.unflatten(tree, leaves)

    half_rows = tokens // lax.axis_size("row")
    hidden_t = hidden.T
    up, down = [cotangent], [cotangent]
    arrived = send(1)
    z = low_and_back(scalars, hidden_t, cotangent, adapter_a, adapter_b)
    moved = lax.ppermute(z, "row", swap)
    down_weight, z = hold((down_weight, z))
    w_ext = load(down_weight, adapter_a)
    z = add_after(z, moved, w_ext)
    def swap_z(z, bit):
        return lax.ppermute(z, "col", [(i, i ^ bit) for i in range(n)])

    def plus(z, moved):
        return (z.astype(jnp.float32) + moved.astype(jnp.float32)).astype(jnp.bfloat16)

    moved, bit = swap_z(z, 1), 2
    arrived, z, moved = hold((arrived, z, moved))
    z = plus(z, moved)
    out, part, waiting = None, None, []
    for k in range(1, n // 2):
        up.append(arrived[0])
        down.append(arrived[1])
        arrived = send(k + 1)
        moved = None
        if 1 < k < n // 2 - 1 and bit < n // 2:
            moved, bit = swap_z(z, bit), bit * 2
        if part is not None:
            waiting.append((part, lax.ppermute(part, "row", swap), places))
        steps, blocks = [(-k, 0), (k, 0)], [up[k], down[k]]
        if k == 1:
            steps, blocks = [(0, 0)] + steps, [far(cotangent)] + blocks
        part = one_pass(n, steps, scalars, w_ext, adapter_b, *blocks)
        places = [(where, i * TILE) for i, (where, _) in enumerate(steps)]
        if k == 2:
            out = join(n, waiting, out, half_rows, w_ext)
            waiting = []
        arrived, part, z, moved, out, waiting = hold((arrived, part, z, moved, out, waiting))
        if moved is not None:
            z = plus(z, moved)
    up.append(arrived[0])
    down.append(arrived[1])
    while bit < n:
        z, bit = plus(z, swap_z(z, bit)), bit * 2
    waiting.append((part, lax.ppermute(part, "row", swap), places))
    part = one_pass(
        n, [(n // 2, 0), (n // 2, half)], scalars, w_ext, adapter_b, up[-1], down[-1]
    )
    part, z, waiting = hold((part, z, waiting))
    waiting.append((part, lax.ppermute(part, "row", swap), [(n // 2, 0)]))
    grad_a = grad_a_of(scalars, z, hidden_t, tenants, rank)
    plan, blocks = [(0, 0)], [cotangent]
    for k in range(1, n // 2 + 1):
        last = k == n // 2
        plan += [(-k, 0), (k, half if last else 0)]
        blocks += [up[k], down[k]]
    grad_b = grad_b_of(n, scalars, z, plan, blocks, cotangent.shape[1] // n, tenants)
    out = join(n, waiting[:-1], out, half_rows)
    out = join(n, waiting[-1:], out, half_rows, in_vmem=True)
    return (
        out.T,
        grad_a.reshape(tenants, rank, ff),
        grad_b.reshape(tenants, rank, -1),
    )


def shards(hidden, cotangent, *rest):
    n, rows = lax.axis_size("col"), cotangent.shape[0]
    if rows == TILE and n % 2 == 0 and n & (n - 1) == 0 and lax.axis_size("row") == 2:
        return ring_shards(hidden, cotangent, *rest)
    return plain_shards(hidden, cotangent, *rest)


def plain_shards(hidden, cotangent, down_weight, adapter_a, adapter_b, seg_start, seg_len, tenant_slot):
    tokens_all = hidden.shape[0]
    local_rows = cotangent.shape[0]
    tile_total = tokens_all // TILE
    tenants = seg_start.shape[0]
    rank_width = adapter_a.shape[1]
    slot_table = (tenant_slot[:, None] == jnp.arange(tenants, dtype=jnp.int32)[None, :]).astype(
        jnp.float32
    )
    tile_first = jnp.arange(tile_total, dtype=jnp.int32) * TILE
    tile_tenant = jnp.sum((tile_first[:, None] >= seg_start[None, :]).astype(jnp.int32), axis=1) - 1
    tenant_hot = (tile_tenant[:, None] == jnp.arange(tenants, dtype=jnp.int32)[None, :]).astype(
        jnp.float32
    )
    tile_slot = jnp.dot(tenant_hot, slot_table, precision=lax.Precision.HIGHEST)
    tenant_slot_rows = jnp.sum(slot_table * seg_len.astype(jnp.float32)[:, None], axis=0)
    tenant_slot_factor = adapter_scale_value / tenant_slot_rows
    offset = lax.axis_index("col") * local_rows
    my_rows = offset + jnp.arange(local_rows, dtype=jnp.int32)
    seg_end = seg_start + seg_len
    live_rows = jnp.any(
        (my_rows[:, None] >= seg_start[None, :]) & (my_rows[:, None] < seg_end[None, :]), axis=1
    )
    masked = jnp.where(live_rows[:, None], cotangent, jnp.zeros_like(cotangent))
    slot_pick = tile_slot.astype(jnp.bfloat16)
    proj_tiles = jnp.einsum(
        "js,srf->jrf", slot_pick, adapter_a, preferred_element_type=jnp.float32
    ).astype(jnp.bfloat16)
    back_tiles = jnp.einsum(
        "js,srd->jrd", slot_pick, adapter_b, preferred_element_type=jnp.float32
    ).astype(jnp.bfloat16)
    hidden_tiles = hidden.reshape(tile_total, TILE, hidden.shape[1])
    low_part = jnp.einsum(
        "jtf,jrf->jtr", hidden_tiles, proj_tiles, preferred_element_type=jnp.float32
    ).reshape(tokens_all, rank_width)
    low_rows = lax.psum(low_part.astype(jnp.bfloat16), "col")
    gathered = lax.all_gather(masked, "col", axis=0, tiled=True)
    grad_part = jnp.einsum(
        "jtd,jrd->jtr",
        gathered.reshape(tile_total, TILE, gathered.shape[1]),
        back_tiles,
        preferred_element_type=jnp.float32,
    ).reshape(tokens_all, rank_width)
    grad_rows = lax.psum(grad_part.astype(jnp.bfloat16), "row")
    half_rows = tokens_all // lax.axis_size("row")
    my_start = lax.axis_index("row") * half_rows
    frozen_path_sum = lax.psum_scatter(
        lax.dot_general(
            gathered, down_weight, (((1,), (1,)), ((), ())), preferred_element_type=jnp.float32
        ).astype(jnp.bfloat16),
        "row",
        scatter_dimension=0,
        tiled=True,
    ).astype(jnp.float32)
    grad_mine = lax.dynamic_slice_in_dim(grad_rows, my_start, half_rows, 0).reshape(
        half_rows // TILE, TILE, rank_width
    )
    proj_mine = lax.dynamic_slice_in_dim(proj_tiles, my_start // TILE, half_rows // TILE, 0)
    adapter_contribution = jnp.einsum(
        "jtr,jrf->jtf", grad_mine, proj_mine, preferred_element_type=jnp.float32
    ).reshape(half_rows, hidden.shape[1])
    hidden_gradient = (frozen_path_sum + adapter_scale_value * adapter_contribution).astype(
        jnp.bfloat16
    )
    grad_tiles = grad_rows.reshape(tile_total, TILE, rank_width)
    first_grad_tiles = jnp.einsum(
        "jtr,jtf->jrf", grad_tiles, hidden_tiles, preferred_element_type=jnp.float32
    )
    grad_a = (
        jnp.einsum("js,jrf->srf", tile_slot, first_grad_tiles, precision=lax.Precision.HIGHEST)
        * tenant_slot_factor[:, None, None]
    )
    col_width = cotangent.shape[1] // lax.axis_size("col")
    col_start = lax.axis_index("col") * col_width
    col_block = lax.dynamic_slice_in_dim(gathered, col_start, col_width, 1).reshape(
        tile_total, TILE, col_width
    )
    second_grad_tiles = jnp.einsum(
        "jtr,jtd->jrd",
        low_rows.reshape(tile_total, TILE, rank_width),
        col_block,
        preferred_element_type=jnp.float32,
    )
    grad_b = (
        jnp.einsum("js,jrd->srd", tile_slot, second_grad_tiles, precision=lax.Precision.HIGHEST)
        * tenant_slot_factor[:, None, None]
    )
    return (hidden_gradient, grad_a, grad_b)


def solution(mesh):
    placed = (
        P("parts", "col"),
        P(("parts", "col"), "row"),
        P("col", "row"),
        P("parts", None, "col"),
        P("parts", None, "row"),
        P("parts"),
        P("parts"),
        P("parts"),
    )
    return jax.shard_map(
        shards,
        mesh=mesh,
        in_specs=placed,
        out_specs=(
            P(("parts", "row"), "col"),
            P("parts", None, "col"),
            P("parts", None, ("row", "col")),
        ),
        check_vma=False,
    )
```

```python
import functools

import jax
import jax.numpy as jnp
from jax import lax
from jax.experimental import pallas as pl
from jax.experimental.pallas import tpu as pltpu
from jax.sharding import PartitionSpec as P

TILE = 128


adapter_scale_value = 4.0

NT = (((1,), (1,)), ((), ()))
MIB = 1 << 20


def far(x):
    return pltpu.with_memory_space_constraint(x, pltpu.HBM)


def near(x):
    return pltpu.with_memory_space_constraint(x, pltpu.VMEM)

LIM = 12
SMALL = pl.CostEstimate(flops=1, bytes_accessed=1, transcendentals=0)


def ring_order(n):
    return [2 * i for i in range(n // 2)] + [2 * i + 1 for i in reversed(range(n // 2))]


def col_at(n, k):
    col = lax.axis_index("col")
    line, side = col // 2, col % 2
    pos = jnp.where(side == 0, line, n - 1 - line)
    pos = lax.rem(pos + k + n, n)
    return jnp.where(pos < n // 2, 2 * pos, 2 * (n - 1 - pos) + 1)


def tile_facts(row0, start, length, slot):
    tenants = start.shape[0]
    found_slot, end = slot[0], start[0] + length[0]
    for i in range(1, tenants):
        here = start[i] <= row0
        found_slot = jnp.where(here, slot[i], found_slot)
        end = jnp.where(here, start[i] + length[i], end)
    return found_slot, end - row0


def put_tile(x_ext, at, data, row0, b_flat, scalars, width, back_out=None):
    rows = data.shape[0]
    tile0 = row0 // TILE * TILE
    slot, live = tile_facts(tile0, *scalars)
    keep = lax.broadcasted_iota(jnp.int32, (rows, 1), 0) < live - (row0 - tile0)
    x_ext[at : at + rows, :width] = jnp.where(keep, data, jnp.zeros_like(data))
    back = lax.dot_general(
        x_ext[at : at + rows, :width], b_flat, NT, preferred_element_type=jnp.float32
    )
    rank = b_flat.shape[0] // scalars[0].shape[0]
    lane = lax.broadcasted_iota(jnp.int32, back.shape, 1)
    mine = (lane >= slot * rank) & (lane < slot * rank + rank)
    spread = jnp.where(mine, back * adapter_scale_value, 0.0).astype(jnp.bfloat16)
    x_ext[at : at + rows, width : width + b_flat.shape[0]] = spread
    pad = x_ext.shape[1] - width - b_flat.shape[0]
    if pad:
        x_ext[at : at + rows, width + b_flat.shape[0] :] = jnp.zeros((rows, pad), jnp.bfloat16)


def low_kernel(start, length, slot, h_hbm, x_hbm, a_ref, b_ref, z_ref, x_ext, low_all, back_all, h_ref, x_ref, sem):
    tenants, rank, ff = a_ref.shape
    flat, width = tenants * rank, b_ref.shape[2]
    x_copy = pltpu.make_async_copy(x_hbm, x_ref, sem.at[0])
    h_copy = pltpu.make_async_copy(h_hbm, h_ref, sem.at[1])
    x_copy.start()
    h_copy.start()
    scalars = (start, length, slot)
    rows = x_ref.shape[0]
    row0 = lax.axis_index("col") * rows
    a_flat = a_ref[...].reshape(flat, ff)
    b_flat = b_ref[...].reshape(flat, width)
    own_slot, live = tile_facts(row0, *scalars)
    keep = lax.broadcasted_iota(jnp.int32, (rows, 1), 0) < live
    x_copy.wait()
    x_ext[...] = jnp.where(keep, x_ref[...], jnp.zeros_like(x_ref))
    back_all[...] = lax.dot_general(b_flat, x_ext[...], NT, preferred_element_type=jnp.float32)
    z_ref[...] = jnp.zeros_like(z_ref)
    z_ref[rank:, pl.ds(pl.multiple_of(row0, TILE), rows)] = back_all[
        pl.ds(pl.multiple_of(own_slot * rank, rank), rank), :
    ]
    h_copy.wait()
    low_all[...] = jnp.dot(a_flat, h_ref[...], preferred_element_type=jnp.float32)
    for j in range(low_all.shape[1] // TILE):
        s, _ = tile_facts(j * TILE, *scalars)
        cols = slice(j * TILE, (j + 1) * TILE)
        z_ref[:rank, cols] = low_all[pl.ds(pl.multiple_of(s * rank, rank), rank), cols] * 0.5


def low_and_back(scalars, hidden_t, cotangent, adapter_a, adapter_b):
    ff, tokens = hidden_t.shape
    rows, width = cotangent.shape
    rank = adapter_a.shape[1]
    flat = adapter_a.shape[0] * rank
    smem = pl.BlockSpec(memory_space=pltpu.SMEM)
    vmem = pl.BlockSpec(memory_space=pltpu.VMEM)
    hbm = pl.BlockSpec(memory_space=pltpu.HBM)
    return pl.pallas_call(
        low_kernel,
        in_specs=[smem, smem, smem, hbm, hbm, vmem, vmem],
        out_specs=vmem,
        out_shape=jax.ShapeDtypeStruct((2 * rank, tokens), jnp.float32),
        scratch_shapes=[
            pltpu.VMEM((rows, width), jnp.bfloat16),
            pltpu.VMEM((flat, tokens), jnp.float32),
            pltpu.VMEM((flat, rows), jnp.float32),
            pltpu.VMEM((ff, tokens), jnp.bfloat16),
            pltpu.VMEM((rows, width), jnp.bfloat16),
            pltpu.SemaphoreType.DMA((2,)),
        ],
        compiler_params=pltpu.CompilerParams(vmem_limit_bytes=LIM * MIB),
        cost_estimate=SMALL,
        name="low_and_back",
    )(*[far(v) for v in scalars], far(hidden_t), far(cotangent), far(adapter_a), far(adapter_b))


def load_kernel(w_hbm, a_ref, w_ext, w_sem):
    ff, width = w_hbm.shape
    pieces = w_sem.shape[0]
    block = ff // pieces
    w_copies = [
        pltpu.make_async_copy(
            w_hbm.at[pl.ds(i * block, block)],
            w_ext.at[pl.ds(i * block, block), pl.ds(0, width)],
            w_sem.at[i],
        )
        for i in range(pieces)
    ]
    for c in w_copies:
        c.start()
    flat = a_ref.shape[0] * a_ref.shape[1]
    w_ext[:, width : width + flat] = a_ref[...].reshape(flat, ff).T
    pad = w_ext.shape[1] - width - flat
    if pad:
        w_ext[:, width + flat :] = jnp.zeros((ff, pad), jnp.bfloat16)
    for c in w_copies:
        c.wait()


def load(down_weight, adapter_a):
    ff, width = down_weight.shape
    flat = adapter_a.shape[0] * adapter_a.shape[1]
    wide = width + -(-flat // 128) * 128
    pieces = 7 if ff % (7 * 16) == 0 else 1
    return pl.pallas_call(
        load_kernel,
        in_specs=[
            pl.BlockSpec(memory_space=pltpu.HBM),
            pl.BlockSpec(memory_space=pltpu.VMEM),
        ],
        out_specs=pl.BlockSpec(memory_space=pltpu.VMEM),
        out_shape=pltpu.VMEM((ff, wide), jnp.bfloat16),
        scratch_shapes=[pltpu.SemaphoreType.DMA((pieces,))],
        compiler_params=pltpu.CompilerParams(vmem_limit_bytes=LIM * MIB),
        cost_estimate=SMALL,
        name="load_weight",
    )(down_weight, far(adapter_a))


def add_kernel(x_ref, y_ref, _, out_ref):
    out_ref[...] = (x_ref[...] + y_ref[...]).astype(out_ref.dtype)


def add_after(x, y, keep):
    vmem = pl.BlockSpec(memory_space=pltpu.VMEM)
    return pl.pallas_call(
        add_kernel,
        in_specs=[vmem, vmem, vmem],
        out_specs=vmem,
        out_shape=jax.ShapeDtypeStruct(x.shape, jnp.bfloat16),
        compiler_params=pltpu.CompilerParams(vmem_limit_bytes=LIM * MIB),
        cost_estimate=SMALL,
        name="add_after",
    )(x, y, near(keep))


def pass_kernel(n, steps, start, length, slot, w_ext, b_ref, *refs):
    xs, p_ref, x_ext = refs[: len(steps)], refs[-2], refs[-1]
    width = b_ref.shape[2]
    flat = b_ref.shape[0] * b_ref.shape[1]
    b_flat = b_ref[...].reshape(flat, width)
    at = 0
    for (k, shift), x_ref in zip(steps, xs):
        row0 = col_at(n, k) * TILE + shift
        put_tile(x_ext, at, x_ref[...], row0, b_flat, (start, length, slot), width)
        at += x_ref.shape[0]
    ff = p_ref.shape[0]
    block = ff // 3
    for i in range(3):
        part = slice(i * block, (i + 1) * block)
        p_ref[part] = lax.dot_general(
            w_ext[part], x_ext[...], NT, preferred_element_type=jnp.float32
        ).astype(jnp.bfloat16)


def one_pass(n, steps, scalars, w_ext, adapter_b, *xs):
    ff, wide = w_ext.shape
    rows = sum(x.shape[0] for x in xs)
    smem = pl.BlockSpec(memory_space=pltpu.SMEM)
    vmem = pl.BlockSpec(memory_space=pltpu.VMEM)
    return pl.pallas_call(
        functools.partial(pass_kernel, n, steps),
        in_specs=[smem, smem, smem] + [vmem] * (2 + len(xs)),
        out_specs=vmem,
        out_shape=jax.ShapeDtypeStruct((ff, rows), jnp.bfloat16),
        scratch_shapes=[pltpu.VMEM((rows, wide), jnp.bfloat16)],
        compiler_params=pltpu.CompilerParams(vmem_limit_bytes=LIM * MIB),
        cost_estimate=SMALL,
        name="part_pass",
    )(*scalars, near(w_ext), adapter_b, *xs)


def outer_rows_kernel(a_ref, b_ref, _, top_ref, bottom_ref):
    half = top_ref.shape[0]
    top_ref[...] = a_ref[:half]
    bottom_ref[...] = b_ref[half:]


def outer_rows(a, b, keep):
    vmem = pl.BlockSpec(memory_space=pltpu.VMEM)
    piece = jax.ShapeDtypeStruct((a.shape[0] // 2, a.shape[1]), a.dtype)
    return pl.pallas_call(
        outer_rows_kernel,
        in_specs=[vmem] * 3,
        out_specs=[vmem] * 2,
        out_shape=[piece] * 2,
        compiler_params=pltpu.CompilerParams(vmem_limit_bytes=LIM * MIB),
        cost_estimate=SMALL,
        name="outer_rows",
    )(a, b, near(keep))


def join_kernel(n, plan, in_vmem, *refs):
    out, parts, sem = refs[-3], refs[-2], refs[-1]
    row = lax.axis_index("row")

    def put_of(i, at):
        return pltpu.make_async_copy(parts.at[i, 0], out.at[:, pl.ds(at, TILE)], sem.at[i, 2])

    def fetch_of(i, own, other):
        return [
            pltpu.make_async_copy(src, parts.at[i, j], sem.at[i, j])
            for j, src in enumerate((own, other))
        ]

    def mine(body):
        for i, (pair, k, lane) in enumerate(plan):
            col = col_at(n, k)
            at = pl.multiple_of(lax.rem(col, n // 2) * TILE, TILE)
            lanes = pl.ds(lane, TILE)
            own, other = refs[2 * pair].at[:, lanes], refs[2 * pair + 1].at[:, lanes]
            pl.when(col // (n // 2) == row)(functools.partial(body, i, own, other, at))

    def begin(i, own, other, at):
        for c in fetch_of(i, own, other):
            c.start()

    def add(i, own, other, at):
        if in_vmem:
            a, b = own[...], other[...]
        else:
            for c in fetch_of(i, own, other):
                c.wait()
            a, b = parts[i, 0], parts[i, 1]
        parts[i, 0] = (a.astype(jnp.float32) + b.astype(jnp.float32)).astype(jnp.bfloat16)
        put_of(i, at).start()

    def end(i, own, other, at):
        put_of(i, at).wait()

    if not in_vmem:
        mine(begin)
    mine(add)
    mine(end)


def join(n, groups, out, half_rows, keep=None, in_vmem=False):
    ff = groups[0][0].shape[0]
    vmem = pl.BlockSpec(memory_space=pltpu.VMEM)
    hbm = pl.BlockSpec(memory_space=pltpu.HBM)
    args, plan, given = [], [], {}
    for pair, (own, other, places) in enumerate(groups):
        args += [own, other]
        plan += [(pair, k, lane) for k, lane in places]
    count = len(args)
    specs = [vmem if in_vmem else pl.BlockSpec(memory_space=pl.ANY)] * count
    if out is not None:
        given = {count: 0}
        args.append(out)
        specs.append(hbm)
    if keep is not None:
        args.append(near(keep))
        specs.append(vmem)

    def body(*refs):
        join_kernel(n, plan, in_vmem, *refs[:count], *refs[len(args) :])

    return pl.pallas_call(
        body,
        in_specs=specs,
        out_specs=hbm,
        out_shape=jax.ShapeDtypeStruct((ff, half_rows), jnp.bfloat16),
        scratch_shapes=[
            pltpu.VMEM((len(plan), 1 if in_vmem else 2, ff, TILE), jnp.bfloat16),
            pltpu.SemaphoreType.DMA((len(plan), 3)),
        ],
        input_output_aliases=given,
        compiler_params=pltpu.CompilerParams(vmem_limit_bytes=LIM * MIB),
        cost_estimate=SMALL,
        name="join_halves",
    )(*args)


def spread_rows(scratch, values, start, length, slot):
    rank = values.shape[0]
    scratch[...] = jnp.zeros_like(scratch)
    for j in range(values.shape[1] // TILE):
        s, _ = tile_facts(j * TILE, start, length, slot)
        cols = slice(j * TILE, (j + 1) * TILE)
        scratch[pl.ds(pl.multiple_of(s * rank, rank), rank), cols] = values[:, cols]


def scale_rows(out_ref, value, start, length, slot):
    rank = value.shape[0] // start.shape[0]
    row_slot = lax.broadcasted_iota(jnp.int32, (value.shape[0], 1), 0) // rank
    factor = jnp.zeros((value.shape[0], 1), jnp.float32)
    for i in range(start.shape[0]):
        one = jnp.full((value.shape[0], 1), length[i], jnp.int32).astype(jnp.float32)
        factor = jnp.where(row_slot == slot[i], adapter_scale_value / one, factor)
    out_ref[...] = value * factor


def grads_kernel(n, plan, start, length, slot, z_ref, h_ref, *refs):
    blocks = refs[: len(plan)]
    out_a, out_ref, spread, x_ref, sem = refs[len(plan) :]
    rank = z_ref.shape[0] // 2
    width = x_ref.shape[1]
    at = pl.multiple_of(lax.axis_index("col") * width, width)
    copies = []
    for i, (k, shift) in enumerate(plan):
        rows = blocks[i].shape[0]
        to = pl.multiple_of(col_at(n, k) * TILE + shift, rows)
        copies.append(
            pltpu.make_async_copy(
                blocks[i].at[:, pl.ds(at, width)], x_ref.at[pl.ds(to, rows)], sem.at[i]
            )
        )
    for c in copies:
        c.start()
    spread_rows(spread, z_ref[:rank].astype(jnp.float32), start, length, slot)
    tokens = spread.shape[1]
    row = lax.broadcasted_iota(jnp.int32, (1, tokens), 1)
    live = row < 0
    for i in range(start.shape[0]):
        live = live | ((row >= start[i]) & (row < start[i] + length[i]))
    low = jnp.where(live, spread[...], 0.0).astype(jnp.bfloat16)
    for c in copies:
        c.wait()
    value = jnp.dot(low, x_ref[...], preferred_element_type=jnp.float32)
    scale_rows(out_ref, value, start, length, slot)
    spread_rows(spread, z_ref[rank:].astype(jnp.float32), start, length, slot)
    value = lax.dot_general(
        spread[...].astype(jnp.bfloat16), h_ref[...], NT, preferred_element_type=jnp.float32
    )
    scale_rows(out_a, value, start, length, slot)


def grads_of(n, scalars, z, hidden_t, plan, blocks, col_width, tenants):
    rank, tokens = z.shape[0] // 2, z.shape[1]
    ff = hidden_t.shape[0]
    smem = pl.BlockSpec(memory_space=pltpu.SMEM)
    vmem = pl.BlockSpec(memory_space=pltpu.VMEM)
    where = pl.BlockSpec(memory_space=pl.ANY)
    return pl.pallas_call(
        functools.partial(grads_kernel, n, plan),
        in_specs=[smem, smem, smem, vmem, vmem] + [where] * len(blocks),
        out_specs=[vmem, vmem],
        out_shape=[
            jax.ShapeDtypeStruct((tenants * rank, ff), jnp.float32),
            jax.ShapeDtypeStruct((tenants * rank, col_width), jnp.float32),
        ],
        scratch_shapes=[
            pltpu.VMEM((tenants * rank, tokens), jnp.float32),
            pltpu.VMEM((tokens, col_width), jnp.bfloat16),
            pltpu.SemaphoreType.DMA((len(blocks),)),
        ],
        compiler_params=pltpu.CompilerParams(vmem_limit_bytes=LIM * MIB),
        cost_estimate=SMALL,
        name="grads",
    )(*scalars, z, hidden_t, *blocks)


def ring_shards(hidden, cotangent, down_weight, adapter_a, adapter_b, seg_start, seg_len, tenant_slot):
    n = lax.axis_size("col")
    tenants, rank = adapter_a.shape[0], adapter_a.shape[1]
    tokens, ff = hidden.shape
    half = cotangent.shape[0] // 2
    scalars = (seg_start, seg_len, tenant_slot)
    order = ring_order(n)
    onward = [(order[i], order[(i + 1) % n]) for i in range(n)]
    back = [(d, s) for s, d in onward]
    swap = [(0, 1), (1, 0)]

    def send(k, w_ext=None):
        u, d = up[-1], down[-1]
        if k == n // 2:
            u, d = outer_rows(u, d, w_ext)
        return lax.ppermute(u, "col", onward), lax.ppermute(d, "col", back)

    def hold(values):
        leaves, tree = jax.tree.flatten(values)
        at = [i for i, v in enumerate(leaves) if hasattr(v, "dtype")]
        held = lax.optimization_barrier([leaves[i] for i in at])
        for i, v in zip(at, held):
            leaves[i] = v
        return jax.tree.unflatten(tree, leaves)

    half_rows = tokens // lax.axis_size("row")
    hidden_t = hidden.T
    up, down = [cotangent], [cotangent]
    arrived = send(1)
    z = low_and_back(scalars, hidden_t, cotangent, adapter_a, adapter_b)
    moved = lax.ppermute(z, "row", swap)
    down_weight, z = hold((down_weight, z))
    w_ext = load(down_weight, adapter_a)
    z = add_after(z, moved, w_ext)
    def swap_z(z, bit):
        return lax.ppermute(z, "col", [(i, i ^ bit) for i in range(n)])

    def plus(z, moved):
        return (z.astype(jnp.float32) + moved.astype(jnp.float32)).astype(jnp.bfloat16)

    moved, bit = swap_z(z, 1), 2
    arrived, z, moved = hold((arrived, z, moved))
    z = plus(z, moved)
    out, part, waiting = None, None, []
    for k in range(1, n // 2):
        up.append(arrived[0])
        down.append(arrived[1])
        arrived = send(k + 1, w_ext)
        moved = None
        if 1 < k < n // 2 - 1 and bit < n // 2:
            moved, bit = swap_z(z, bit), bit * 2
        if part is not None:
            waiting.append((part, lax.ppermute(part, "row", swap), places))
        steps, blocks = [(-k, 0), (k, 0)], [up[k], down[k]]
        if k == 1:
            steps, blocks = [(0, 0)] + steps, [far(cotangent)] + blocks
        part = one_pass(n, steps, scalars, w_ext, adapter_b, *blocks)
        places = [(where, i * TILE) for i, (where, _) in enumerate(steps)]
        if k >= 2:
            out = join(n, waiting, out, half_rows, w_ext)
            waiting = []
        arrived, part, z, moved, out, waiting = hold((arrived, part, z, moved, out, waiting))
        if moved is not None:
            z = plus(z, moved)
    up.append(arrived[0])
    down.append(arrived[1])
    while bit < n:
        z, bit = plus(z, swap_z(z, bit)), bit * 2
    waiting.append((part, lax.ppermute(part, "row", swap), places))
    part = one_pass(
        n, [(n // 2, 0), (n // 2, half)], scalars, w_ext, adapter_b, up[-1], down[-1]
    )
    part, z, waiting = hold((part, z, waiting))
    waiting.append((part, lax.ppermute(part, "row", swap), [(n // 2, 0)]))
    plan, blocks = [(0, 0)], [cotangent]
    for k in range(1, n // 2 + 1):
        last = k == n // 2
        plan += [(-k, 0), (k, half if last else 0)]
        blocks += [up[k], down[k]]
    grad_a, grad_b = grads_of(
        n, scalars, z, hidden_t, plan, blocks, cotangent.shape[1] // n, tenants
    )
    out = join(n, waiting[:-1], out, half_rows)
    out = join(n, waiting[-1:], out, half_rows, in_vmem=True)
    return (
        out.T,
        grad_a.reshape(tenants, rank, ff),
        grad_b.reshape(tenants, rank, -1),
    )


def shards(hidden, cotangent, *rest):
    n, rows = lax.axis_size("col"), cotangent.shape[0]
    if rows == TILE and n % 2 == 0 and n & (n - 1) == 0 and lax.axis_size("row") == 2:
        return ring_shards(hidden, cotangent, *rest)
    return plain_shards(hidden, cotangent, *rest)


def plain_shards(hidden, cotangent, down_weight, adapter_a, adapter_b, seg_start, seg_len, tenant_slot):
    tokens_all = hidden.shape[0]
    local_rows = cotangent.shape[0]
    tile_total = tokens_all // TILE
    tenants = seg_start.shape[0]
    rank_width = adapter_a.shape[1]
    slot_table = (tenant_slot[:, None] == jnp.arange(tenants, dtype=jnp.int32)[None, :]).astype(
        jnp.float32
    )
    tile_first = jnp.arange(tile_total, dtype=jnp.int32) * TILE
    tile_tenant = jnp.sum((tile_first[:, None] >= seg_start[None, :]).astype(jnp.int32), axis=1) - 1
    tenant_hot = (tile_tenant[:, None] == jnp.arange(tenants, dtype=jnp.int32)[None, :]).astype(
        jnp.float32
    )
    tile_slot = jnp.dot(tenant_hot, slot_table, precision=lax.Precision.HIGHEST)
    tenant_slot_rows = jnp.sum(slot_table * seg_len.astype(jnp.float32)[:, None], axis=0)
    tenant_slot_factor = adapter_scale_value / tenant_slot_rows
    offset = lax.axis_index("col") * local_rows
    my_rows = offset + jnp.arange(local_rows, dtype=jnp.int32)
    seg_end = seg_start + seg_len
    live_rows = jnp.any(
        (my_rows[:, None] >= seg_start[None, :]) & (my_rows[:, None] < seg_end[None, :]), axis=1
    )
    masked = jnp.where(live_rows[:, None], cotangent, jnp.zeros_like(cotangent))
    slot_pick = tile_slot.astype(jnp.bfloat16)
    proj_tiles = jnp.einsum(
        "js,srf->jrf", slot_pick, adapter_a, preferred_element_type=jnp.float32
    ).astype(jnp.bfloat16)
    back_tiles = jnp.einsum(
        "js,srd->jrd", slot_pick, adapter_b, preferred_element_type=jnp.float32
    ).astype(jnp.bfloat16)
    hidden_tiles = hidden.reshape(tile_total, TILE, hidden.shape[1])
    low_part = jnp.einsum(
        "jtf,jrf->jtr", hidden_tiles, proj_tiles, preferred_element_type=jnp.float32
    ).reshape(tokens_all, rank_width)
    low_rows = lax.psum(low_part.astype(jnp.bfloat16), "col")
    gathered = lax.all_gather(masked, "col", axis=0, tiled=True)
    grad_part = jnp.einsum(
        "jtd,jrd->jtr",
        gathered.reshape(tile_total, TILE, gathered.shape[1]),
        back_tiles,
        preferred_element_type=jnp.float32,
    ).reshape(tokens_all, rank_width)
    grad_rows = lax.psum(grad_part.astype(jnp.bfloat16), "row")
    half_rows = tokens_all // lax.axis_size("row")
    my_start = lax.axis_index("row") * half_rows
    frozen_path_sum = lax.psum_scatter(
        lax.dot_general(
            gathered, down_weight, (((1,), (1,)), ((), ())), preferred_element_type=jnp.float32
        ).astype(jnp.bfloat16),
        "row",
        scatter_dimension=0,
        tiled=True,
    ).astype(jnp.float32)
    grad_mine = lax.dynamic_slice_in_dim(grad_rows, my_start, half_rows, 0).reshape(
        half_rows // TILE, TILE, rank_width
    )
    proj_mine = lax.dynamic_slice_in_dim(proj_tiles, my_start // TILE, half_rows // TILE, 0)
    adapter_contribution = jnp.einsum(
        "jtr,jrf->jtf", grad_mine, proj_mine, preferred_element_type=jnp.float32
    ).reshape(half_rows, hidden.shape[1])
    hidden_gradient = (frozen_path_sum + adapter_scale_value * adapter_contribution).astype(
        jnp.bfloat16
    )
    grad_tiles = grad_rows.reshape(tile_total, TILE, rank_width)
    first_grad_tiles = jnp.einsum(
        "jtr,jtf->jrf", grad_tiles, hidden_tiles, preferred_element_type=jnp.float32
    )
    grad_a = (
        jnp.einsum("js,jrf->srf", tile_slot, first_grad_tiles, precision=lax.Precision.HIGHEST)
        * tenant_slot_factor[:, None, None]
    )
    col_width = cotangent.shape[1] // lax.axis_size("col")
    col_start = lax.axis_index("col") * col_width
    col_block = lax.dynamic_slice_in_dim(gathered, col_start, col_width, 1).reshape(
        tile_total, TILE, col_width
    )
    second_grad_tiles = jnp.einsum(
        "jtr,jtd->jrd",
        low_rows.reshape(tile_total, TILE, rank_width),
        col_block,
        preferred_element_type=jnp.float32,
    )
    grad_b = (
        jnp.einsum("js,jrd->srd", tile_slot, second_grad_tiles, precision=lax.Precision.HIGHEST)
        * tenant_slot_factor[:, None, None]
    )
    return (hidden_gradient, grad_a, grad_b)


def solution(mesh):
    placed = (
        P("parts", "col"),
        P(("parts", "col"), "row"),
        P("col", "row"),
        P("parts", None, "col"),
        P("parts", None, "row"),
        P("parts"),
        P("parts"),
        P("parts"),
    )
    return jax.shard_map(
        shards,
        mesh=mesh,
        in_specs=placed,
        out_specs=(
            P(("parts", "row"), "col"),
            P("parts", None, "col"),
            P("parts", None, ("row", "col")),
        ),
        check_vma=False,
    )
```

```python
import functools

import jax
import jax.numpy as jnp
from jax import lax
from jax.experimental import pallas as pl
from jax.experimental.pallas import tpu as pltpu
from jax.sharding import PartitionSpec as P

TILE = 128


adapter_scale_value = 4.0

NT = (((1,), (1,)), ((), ()))
MIB = 1 << 20


def far(x):
    return pltpu.with_memory_space_constraint(x, pltpu.HBM)


def near(x):
    return pltpu.with_memory_space_constraint(x, pltpu.VMEM)

LIM = 12
SMALL = pl.CostEstimate(flops=1, bytes_accessed=1, transcendentals=0)


def ring_order(n):
    return [2 * i for i in range(n // 2)] + [2 * i + 1 for i in reversed(range(n // 2))]


def col_at(n, k):
    col = lax.axis_index("col")
    line, side = col // 2, col % 2
    pos = jnp.where(side == 0, line, n - 1 - line)
    pos = lax.rem(pos + k + n, n)
    return jnp.where(pos < n // 2, 2 * pos, 2 * (n - 1 - pos) + 1)


def tile_facts(row0, start, length, slot):
    tenants = start.shape[0]
    found_slot, end = slot[0], start[0] + length[0]
    for i in range(1, tenants):
        here = start[i] <= row0
        found_slot = jnp.where(here, slot[i], found_slot)
        end = jnp.where(here, start[i] + length[i], end)
    return found_slot, end - row0


def put_tile(x_ext, at, data, row0, b_flat, scalars, width, back_out=None):
    rows = data.shape[0]
    tile0 = row0 // TILE * TILE
    slot, live = tile_facts(tile0, *scalars)
    keep = lax.broadcasted_iota(jnp.int32, (rows, 1), 0) < live - (row0 - tile0)
    x_ext[at : at + rows, :width] = jnp.where(keep, data, jnp.zeros_like(data))
    back = lax.dot_general(
        x_ext[at : at + rows, :width], b_flat, NT, preferred_element_type=jnp.float32
    )
    rank = b_flat.shape[0] // scalars[0].shape[0]
    lane = lax.broadcasted_iota(jnp.int32, back.shape, 1)
    mine = (lane >= slot * rank) & (lane < slot * rank + rank)
    spread = jnp.where(mine, back * adapter_scale_value, 0.0).astype(jnp.bfloat16)
    x_ext[at : at + rows, width : width + b_flat.shape[0]] = spread
    pad = x_ext.shape[1] - width - b_flat.shape[0]
    if pad:
        x_ext[at : at + rows, width + b_flat.shape[0] :] = jnp.zeros((rows, pad), jnp.bfloat16)


def low_kernel(start, length, slot, h_hbm, x_hbm, a_ref, b_ref, z_ref, x_ext, low_all, back_all, h_ref, x_ref, sem):
    tenants, rank, ff = a_ref.shape
    flat, width = tenants * rank, b_ref.shape[2]
    x_copy = pltpu.make_async_copy(x_hbm, x_ref, sem.at[0])
    h_copy = pltpu.make_async_copy(h_hbm, h_ref, sem.at[1])
    x_copy.start()
    h_copy.start()
    scalars = (start, length, slot)
    rows = x_ref.shape[0]
    row0 = lax.axis_index("col") * rows
    a_flat = a_ref[...].reshape(flat, ff)
    b_flat = b_ref[...].reshape(flat, width)
    own_slot, live = tile_facts(row0, *scalars)
    keep = lax.broadcasted_iota(jnp.int32, (rows, 1), 0) < live
    x_copy.wait()
    x_ext[...] = jnp.where(keep, x_ref[...], jnp.zeros_like(x_ref))
    back_all[...] = lax.dot_general(b_flat, x_ext[...], NT, preferred_element_type=jnp.float32)
    z_ref[...] = jnp.zeros_like(z_ref)
    z_ref[rank:, pl.ds(pl.multiple_of(row0, TILE), rows)] = back_all[
        pl.ds(pl.multiple_of(own_slot * rank, rank), rank), :
    ]
    h_copy.wait()
    low_all[...] = jnp.dot(a_flat, h_ref[...], preferred_element_type=jnp.float32)
    for j in range(low_all.shape[1] // TILE):
        s, _ = tile_facts(j * TILE, *scalars)
        cols = slice(j * TILE, (j + 1) * TILE)
        z_ref[:rank, cols] = low_all[pl.ds(pl.multiple_of(s * rank, rank), rank), cols] * 0.5


def low_and_back(scalars, hidden_t, cotangent, adapter_a, adapter_b):
    ff, tokens = hidden_t.shape
    rows, width = cotangent.shape
    rank = adapter_a.shape[1]
    flat = adapter_a.shape[0] * rank
    smem = pl.BlockSpec(memory_space=pltpu.SMEM)
    vmem = pl.BlockSpec(memory_space=pltpu.VMEM)
    hbm = pl.BlockSpec(memory_space=pltpu.HBM)
    return pl.pallas_call(
        low_kernel,
        in_specs=[smem, smem, smem, hbm, hbm, vmem, vmem],
        out_specs=vmem,
        out_shape=jax.ShapeDtypeStruct((2 * rank, tokens), jnp.float32),
        scratch_shapes=[
            pltpu.VMEM((rows, width), jnp.bfloat16),
            pltpu.VMEM((flat, tokens), jnp.float32),
            pltpu.VMEM((flat, rows), jnp.float32),
            pltpu.VMEM((ff, tokens), jnp.bfloat16),
            pltpu.VMEM((rows, width), jnp.bfloat16),
            pltpu.SemaphoreType.DMA((2,)),
        ],
        compiler_params=pltpu.CompilerParams(vmem_limit_bytes=LIM * MIB),
        cost_estimate=SMALL,
        name="low_and_back",
    )(*[far(v) for v in scalars], far(hidden_t), far(cotangent), far(adapter_a), far(adapter_b))


def load_kernel(w_hbm, a_ref, w_ext, w_sem):
    ff, width = w_hbm.shape
    pieces = w_sem.shape[0]
    block = ff // pieces
    w_copies = [
        pltpu.make_async_copy(
            w_hbm.at[pl.ds(i * block, block)],
            w_ext.at[pl.ds(i * block, block), pl.ds(0, width)],
            w_sem.at[i],
        )
        for i in range(pieces)
    ]
    for c in w_copies:
        c.start()
    flat = a_ref.shape[0] * a_ref.shape[1]
    w_ext[:, width : width + flat] = a_ref[...].reshape(flat, ff).T
    pad = w_ext.shape[1] - width - flat
    if pad:
        w_ext[:, width + flat :] = jnp.zeros((ff, pad), jnp.bfloat16)
    for c in w_copies:
        c.wait()


def load(down_weight, adapter_a):
    ff, width = down_weight.shape
    flat = adapter_a.shape[0] * adapter_a.shape[1]
    wide = width + -(-flat // 128) * 128
    pieces = 7 if ff % (7 * 16) == 0 else 1
    return pl.pallas_call(
        load_kernel,
        in_specs=[
            pl.BlockSpec(memory_space=pltpu.HBM),
            pl.BlockSpec(memory_space=pltpu.VMEM),
        ],
        out_specs=pl.BlockSpec(memory_space=pltpu.VMEM),
        out_shape=pltpu.VMEM((ff, wide), jnp.bfloat16),
        scratch_shapes=[pltpu.SemaphoreType.DMA((pieces,))],
        compiler_params=pltpu.CompilerParams(vmem_limit_bytes=LIM * MIB),
        cost_estimate=SMALL,
        name="load_weight",
    )(down_weight, far(adapter_a))


def add_kernel(x_ref, y_ref, _, out_ref):
    out_ref[...] = (x_ref[...] + y_ref[...]).astype(out_ref.dtype)


def add_after(x, y, keep):
    vmem = pl.BlockSpec(memory_space=pltpu.VMEM)
    return pl.pallas_call(
        add_kernel,
        in_specs=[vmem, vmem, vmem],
        out_specs=vmem,
        out_shape=jax.ShapeDtypeStruct(x.shape, jnp.bfloat16),
        compiler_params=pltpu.CompilerParams(vmem_limit_bytes=LIM * MIB),
        cost_estimate=SMALL,
        name="add_after",
    )(x, y, near(keep))


def pass_kernel(n, steps, start, length, slot, w_ext, b_ref, *refs):
    xs, p_ref, x_ext = refs[: len(steps)], refs[-2], refs[-1]
    width = b_ref.shape[2]
    flat = b_ref.shape[0] * b_ref.shape[1]
    b_flat = b_ref[...].reshape(flat, width)
    at = 0
    for (k, shift), x_ref in zip(steps, xs):
        row0 = col_at(n, k) * TILE + shift
        put_tile(x_ext, at, x_ref[...], row0, b_flat, (start, length, slot), width)
        at += x_ref.shape[0]
    ff = p_ref.shape[0]
    block = ff // 3
    for i in range(3):
        part = slice(i * block, (i + 1) * block)
        p_ref[part] = lax.dot_general(
            w_ext[part], x_ext[...], NT, preferred_element_type=jnp.float32
        ).astype(jnp.bfloat16)


def one_pass(n, steps, scalars, w_ext, adapter_b, *xs):
    ff, wide = w_ext.shape
    rows = sum(x.shape[0] for x in xs)
    smem = pl.BlockSpec(memory_space=pltpu.SMEM)
    vmem = pl.BlockSpec(memory_space=pltpu.VMEM)
    return pl.pallas_call(
        functools.partial(pass_kernel, n, steps),
        in_specs=[smem, smem, smem] + [vmem] * (2 + len(xs)),
        out_specs=vmem,
        out_shape=jax.ShapeDtypeStruct((ff, rows), jnp.bfloat16),
        scratch_shapes=[pltpu.VMEM((rows, wide), jnp.bfloat16)],
        compiler_params=pltpu.CompilerParams(vmem_limit_bytes=LIM * MIB),
        cost_estimate=SMALL,
        name="part_pass",
    )(*scalars, near(w_ext), adapter_b, *xs)


def outer_rows_kernel(a_ref, b_ref, _, top_ref, bottom_ref):
    half = top_ref.shape[0]
    top_ref[...] = a_ref[:half]
    bottom_ref[...] = b_ref[half:]


def outer_rows(a, b, keep):
    vmem = pl.BlockSpec(memory_space=pltpu.VMEM)
    piece = jax.ShapeDtypeStruct((a.shape[0] // 2, a.shape[1]), a.dtype)
    return pl.pallas_call(
        outer_rows_kernel,
        in_specs=[vmem] * 3,
        out_specs=[vmem] * 2,
        out_shape=[piece] * 2,
        compiler_params=pltpu.CompilerParams(vmem_limit_bytes=LIM * MIB),
        cost_estimate=SMALL,
        name="outer_rows",
    )(a, b, near(keep))


def join_kernel(n, plan, in_vmem, *refs):
    out, parts, sem = refs[-3], refs[-2], refs[-1]
    row = lax.axis_index("row")

    def put_of(i, at):
        return pltpu.make_async_copy(parts.at[i, 0], out.at[:, pl.ds(at, TILE)], sem.at[i, 2])

    def fetch_of(i, own, other):
        return [
            pltpu.make_async_copy(src, parts.at[i, j], sem.at[i, j])
            for j, src in enumerate((own, other))
        ]

    def mine(body):
        for i, (pair, k, lane) in enumerate(plan):
            col = col_at(n, k)
            at = pl.multiple_of(lax.rem(col, n // 2) * TILE, TILE)
            lanes = pl.ds(lane, TILE)
            own, other = refs[2 * pair].at[:, lanes], refs[2 * pair + 1].at[:, lanes]
            pl.when(col // (n // 2) == row)(functools.partial(body, i, own, other, at))

    def begin(i, own, other, at):
        for c in fetch_of(i, own, other):
            c.start()

    def add(i, own, other, at):
        if in_vmem:
            a, b = own[...], other[...]
        else:
            for c in fetch_of(i, own, other):
                c.wait()
            a, b = parts[i, 0], parts[i, 1]
        parts[i, 0] = (a.astype(jnp.float32) + b.astype(jnp.float32)).astype(jnp.bfloat16)
        put_of(i, at).start()

    def end(i, own, other, at):
        put_of(i, at).wait()

    if not in_vmem:
        mine(begin)
    mine(add)
    mine(end)


def join(n, groups, out, half_rows, keep=None, in_vmem=False):
    ff = groups[0][0].shape[0]
    vmem = pl.BlockSpec(memory_space=pltpu.VMEM)
    hbm = pl.BlockSpec(memory_space=pltpu.HBM)
    args, plan, given = [], [], {}
    for pair, (own, other, places) in enumerate(groups):
        args += [own, other]
        plan += [(pair, k, lane) for k, lane in places]
    count = len(args)
    specs = [vmem if in_vmem else pl.BlockSpec(memory_space=pl.ANY)] * count
    if out is not None:
        given = {count: 0}
        args.append(out)
        specs.append(hbm)
    if keep is not None:
        args.append(near(keep))
        specs.append(vmem)

    def body(*refs):
        join_kernel(n, plan, in_vmem, *refs[:count], *refs[len(args) :])

    return pl.pallas_call(
        body,
        in_specs=specs,
        out_specs=hbm,
        out_shape=jax.ShapeDtypeStruct((ff, half_rows), jnp.bfloat16),
        scratch_shapes=[
            pltpu.VMEM((len(plan), 1 if in_vmem else 2, ff, TILE), jnp.bfloat16),
            pltpu.SemaphoreType.DMA((len(plan), 3)),
        ],
        input_output_aliases=given,
        compiler_params=pltpu.CompilerParams(vmem_limit_bytes=LIM * MIB),
        cost_estimate=SMALL,
        name="join_halves",
    )(*args)


def spread_rows(scratch, values, start, length, slot):
    rank = values.shape[0]
    scratch[...] = jnp.zeros_like(scratch)
    for j in range(values.shape[1] // TILE):
        s, _ = tile_facts(j * TILE, start, length, slot)
        cols = slice(j * TILE, (j + 1) * TILE)
        scratch[pl.ds(pl.multiple_of(s * rank, rank), rank), cols] = values[:, cols]


def scale_rows(out_ref, value, start, length, slot):
    rank = value.shape[0] // start.shape[0]
    row_slot = lax.broadcasted_iota(jnp.int32, (value.shape[0], 1), 0) // rank
    factor = jnp.zeros((value.shape[0], 1), jnp.float32)
    for i in range(start.shape[0]):
        one = jnp.full((value.shape[0], 1), length[i], jnp.int32).astype(jnp.float32)
        factor = jnp.where(row_slot == slot[i], adapter_scale_value / one, factor)
    out_ref[...] = value * factor


def grads_kernel(n, plan, start, length, slot, z_ref, h_ref, *refs):
    blocks = refs[: len(plan)]
    out_a, out_ref, spread, x_ref, sem = refs[len(plan) :]
    rank = z_ref.shape[0] // 2
    width = x_ref.shape[1]
    at = pl.multiple_of(lax.axis_index("col") * width, width)
    copies = []
    for i, (k, shift) in enumerate(plan):
        rows = blocks[i].shape[0]
        to = pl.multiple_of(col_at(n, k) * TILE + shift, rows)
        copies.append(
            pltpu.make_async_copy(
                blocks[i].at[:, pl.ds(at, width)], x_ref.at[pl.ds(to, rows)], sem.at[i]
            )
        )
    for c in copies:
        c.start()
    spread_rows(spread, z_ref[:rank].astype(jnp.float32), start, length, slot)
    tokens = spread.shape[1]
    row = lax.broadcasted_iota(jnp.int32, (1, tokens), 1)
    live = row < 0
    for i in range(start.shape[0]):
        live = live | ((row >= start[i]) & (row < start[i] + length[i]))
    low = jnp.where(live, spread[...], 0.0).astype(jnp.bfloat16)
    for c in copies:
        c.wait()
    value = jnp.dot(low, x_ref[...], preferred_element_type=jnp.float32)
    scale_rows(out_ref, value, start, length, slot)
    spread_rows(spread, z_ref[rank:].astype(jnp.float32), start, length, slot)
    value = lax.dot_general(
        spread[...].astype(jnp.bfloat16), h_ref[...], NT, preferred_element_type=jnp.float32
    )
    scale_rows(out_a, value, start, length, slot)


def grads_of(n, scalars, z, hidden_t, plan, blocks, col_width, tenants):
    rank, tokens = z.shape[0] // 2, z.shape[1]
    ff = hidden_t.shape[0]
    smem = pl.BlockSpec(memory_space=pltpu.SMEM)
    vmem = pl.BlockSpec(memory_space=pltpu.VMEM)
    where = pl.BlockSpec(memory_space=pl.ANY)
    return pl.pallas_call(
        functools.partial(grads_kernel, n, plan),
        in_specs=[smem, smem, smem, vmem, vmem] + [where] * len(blocks),
        out_specs=[vmem, vmem],
        out_shape=[
            jax.ShapeDtypeStruct((tenants * rank, ff), jnp.float32),
            jax.ShapeDtypeStruct((tenants * rank, col_width), jnp.float32),
        ],
        scratch_shapes=[
            pltpu.VMEM((tenants * rank, tokens), jnp.float32),
            pltpu.VMEM((tokens, col_width), jnp.bfloat16),
            pltpu.SemaphoreType.DMA((len(blocks),)),
        ],
        compiler_params=pltpu.CompilerParams(vmem_limit_bytes=LIM * MIB),
        cost_estimate=SMALL,
        name="grads",
    )(*scalars, z, hidden_t, *blocks)


def ring_shards(hidden, cotangent, down_weight, adapter_a, adapter_b, seg_start, seg_len, tenant_slot):
    n = lax.axis_size("col")
    tenants, rank = adapter_a.shape[0], adapter_a.shape[1]
    tokens, ff = hidden.shape
    half = cotangent.shape[0] // 2
    scalars = (seg_start, seg_len, tenant_slot)
    order = ring_order(n)
    onward = [(order[i], order[(i + 1) % n]) for i in range(n)]
    back = [(d, s) for s, d in onward]
    swap = [(0, 1), (1, 0)]

    def send(k, w_ext=None):
        u, d = up[-1], down[-1]
        if k == n // 2:
            u, d = outer_rows(u, d, w_ext)
        return lax.ppermute(u, "col", onward), lax.ppermute(d, "col", back)

    def hold(values):
        leaves, tree = jax.tree.flatten(values)
        at = [i for i, v in enumerate(leaves) if hasattr(v, "dtype")]
        held = lax.optimization_barrier([leaves[i] for i in at])
        for i, v in zip(at, held):
            leaves[i] = v
        return jax.tree.unflatten(tree, leaves)

    half_rows = tokens // lax.axis_size("row")
    hidden_t = hidden.T
    up, down = [cotangent], [cotangent]
    arrived = send(1)
    z = low_and_back(scalars, hidden_t, cotangent, adapter_a, adapter_b)
    moved = lax.ppermute(z, "row", swap)
    down_weight, z = hold((down_weight, z))
    w_ext = load(down_weight, adapter_a)
    z = add_after(z, moved, w_ext)
    def swap_z(z, bit):
        return lax.ppermute(z, "col", [(i, i ^ bit) for i in range(n)])

    def plus(z, moved):
        return (z.astype(jnp.float32) + moved.astype(jnp.float32)).astype(jnp.bfloat16)

    moved, bit = swap_z(z, 1), 2
    arrived, z = hold((arrived, z))
    z = plus(z, moved)
    out, part, waiting = None, None, []
    for k in range(1, n // 2):
        up.append(arrived[0])
        down.append(arrived[1])
        arrived = send(k + 1, w_ext)
        moved = None
        if 1 < k < n // 2 - 1 and bit < n // 2:
            moved, bit = swap_z(z, bit), bit * 2
        if part is not None:
            waiting.append((part, lax.ppermute(part, "row", swap), places))
        steps, blocks = [(-k, 0), (k, 0)], [up[k], down[k]]
        if k == 1:
            steps, blocks = [(0, 0)] + steps, [far(cotangent)] + blocks
        part = one_pass(n, steps, scalars, w_ext, adapter_b, *blocks)
        places = [(where, i * TILE) for i, (where, _) in enumerate(steps)]
        if k >= 2:
            out = join(n, waiting, out, half_rows, w_ext)
            waiting = []
        arrived, part, z, moved, out, waiting = hold((arrived, part, z, moved, out, waiting))
        if moved is not None:
            z = plus(z, moved)
    up.append(arrived[0])
    down.append(arrived[1])
    while bit < n:
        z, bit = plus(z, swap_z(z, bit)), bit * 2
    waiting.append((part, lax.ppermute(part, "row", swap), places))
    part = one_pass(
        n, [(n // 2, 0), (n // 2, half)], scalars, w_ext, adapter_b, up[-1], down[-1]
    )
    part, z, waiting = hold((part, z, waiting))
    waiting.append((part, lax.ppermute(part, "row", swap), [(n // 2, 0)]))
    plan, blocks = [(0, 0)], [cotangent]
    for k in range(1, n // 2 + 1):
        last = k == n // 2
        plan += [(-k, 0), (k, half if last else 0)]
        blocks += [up[k], down[k]]
    grad_a, grad_b = grads_of(
        n, scalars, z, hidden_t, plan, blocks, cotangent.shape[1] // n, tenants
    )
    out = join(n, waiting, out, half_rows)
    return (
        out.T,
        grad_a.reshape(tenants, rank, ff),
        grad_b.reshape(tenants, rank, -1),
    )


def shards(hidden, cotangent, *rest):
    n, rows = lax.axis_size("col"), cotangent.shape[0]
    if rows == TILE and n % 2 == 0 and n & (n - 1) == 0 and lax.axis_size("row") == 2:
        return ring_shards(hidden, cotangent, *rest)
    return plain_shards(hidden, cotangent, *rest)


def plain_shards(hidden, cotangent, down_weight, adapter_a, adapter_b, seg_start, seg_len, tenant_slot):
    tokens_all = hidden.shape[0]
    local_rows = cotangent.shape[0]
    tile_total = tokens_all // TILE
    tenants = seg_start.shape[0]
    rank_width = adapter_a.shape[1]
    slot_table = (tenant_slot[:, None] == jnp.arange(tenants, dtype=jnp.int32)[None, :]).astype(
        jnp.float32
    )
    tile_first = jnp.arange(tile_total, dtype=jnp.int32) * TILE
    tile_tenant = jnp.sum((tile_first[:, None] >= seg_start[None, :]).astype(jnp.int32), axis=1) - 1
    tenant_hot = (tile_tenant[:, None] == jnp.arange(tenants, dtype=jnp.int32)[None, :]).astype(
        jnp.float32
    )
    tile_slot = jnp.dot(tenant_hot, slot_table, precision=lax.Precision.HIGHEST)
    tenant_slot_rows = jnp.sum(slot_table * seg_len.astype(jnp.float32)[:, None], axis=0)
    tenant_slot_factor = adapter_scale_value / tenant_slot_rows
    offset = lax.axis_index("col") * local_rows
    my_rows = offset + jnp.arange(local_rows, dtype=jnp.int32)
    seg_end = seg_start + seg_len
    live_rows = jnp.any(
        (my_rows[:, None] >= seg_start[None, :]) & (my_rows[:, None] < seg_end[None, :]), axis=1
    )
    masked = jnp.where(live_rows[:, None], cotangent, jnp.zeros_like(cotangent))
    slot_pick = tile_slot.astype(jnp.bfloat16)
    proj_tiles = jnp.einsum(
        "js,srf->jrf", slot_pick, adapter_a, preferred_element_type=jnp.float32
    ).astype(jnp.bfloat16)
    back_tiles = jnp.einsum(
        "js,srd->jrd", slot_pick, adapter_b, preferred_element_type=jnp.float32
    ).astype(jnp.bfloat16)
    hidden_tiles = hidden.reshape(tile_total, TILE, hidden.shape[1])
    low_part = jnp.einsum(
        "jtf,jrf->jtr", hidden_tiles, proj_tiles, preferred_element_type=jnp.float32
    ).reshape(tokens_all, rank_width)
    low_rows = lax.psum(low_part.astype(jnp.bfloat16), "col")
    gathered = lax.all_gather(masked, "col", axis=0, tiled=True)
    grad_part = jnp.einsum(
        "jtd,jrd->jtr",
        gathered.reshape(tile_total, TILE, gathered.shape[1]),
        back_tiles,
        preferred_element_type=jnp.float32,
    ).reshape(tokens_all, rank_width)
    grad_rows = lax.psum(grad_part.astype(jnp.bfloat16), "row")
    half_rows = tokens_all // lax.axis_size("row")
    my_start = lax.axis_index("row") * half_rows
    frozen_path_sum = lax.psum_scatter(
        lax.dot_general(
            gathered, down_weight, (((1,), (1,)), ((), ())), preferred_element_type=jnp.float32
        ).astype(jnp.bfloat16),
        "row",
        scatter_dimension=0,
        tiled=True,
    ).astype(jnp.float32)
    grad_mine = lax.dynamic_slice_in_dim(grad_rows, my_start, half_rows, 0).reshape(
        half_rows // TILE, TILE, rank_width
    )
    proj_mine = lax.dynamic_slice_in_dim(proj_tiles, my_start // TILE, half_rows // TILE, 0)
    adapter_contribution = jnp.einsum(
        "jtr,jrf->jtf", grad_mine, proj_mine, preferred_element_type=jnp.float32
    ).reshape(half_rows, hidden.shape[1])
    hidden_gradient = (frozen_path_sum + adapter_scale_value * adapter_contribution).astype(
        jnp.bfloat16
    )
    grad_tiles = grad_rows.reshape(tile_total, TILE, rank_width)
    first_grad_tiles = jnp.einsum(
        "jtr,jtf->jrf", grad_tiles, hidden_tiles, preferred_element_type=jnp.float32
    )
    grad_a = (
        jnp.einsum("js,jrf->srf", tile_slot, first_grad_tiles, precision=lax.Precision.HIGHEST)
        * tenant_slot_factor[:, None, None]
    )
    col_width = cotangent.shape[1] // lax.axis_size("col")
    col_start = lax.axis_index("col") * col_width
    col_block = lax.dynamic_slice_in_dim(gathered, col_start, col_width, 1).reshape(
        tile_total, TILE, col_width
    )
    second_grad_tiles = jnp.einsum(
        "jtr,jtd->jrd",
        low_rows.reshape(tile_total, TILE, rank_width),
        col_block,
        preferred_element_type=jnp.float32,
    )
    grad_b = (
        jnp.einsum("js,jrd->srd", tile_slot, second_grad_tiles, precision=lax.Precision.HIGHEST)
        * tenant_slot_factor[:, None, None]
    )
    return (hidden_gradient, grad_a, grad_b)


def solution(mesh):
    placed = (
        P("parts", "col"),
        P(("parts", "col"), "row"),
        P("col", "row"),
        P("parts", None, "col"),
        P("parts", None, "row"),
        P("parts"),
        P("parts"),
        P("parts"),
    )
    return jax.shard_map(
        shards,
        mesh=mesh,
        in_specs=placed,
        out_specs=(
            P(("parts", "row"), "col"),
            P("parts", None, "col"),
            P("parts", None, ("row", "col")),
        ),
        check_vma=False,
    )
```
